32 devices in a mesh: groups: 2 (over x), loop: 4 (over y, core), width: 4 (over z).
Axes of the slice: x: 2, y: 2, z: 4, core: 2. Of those that a mesh axis runs over, the one named last changes fastest.
Arguments:
- inputs: bfloat16 [384, 8192], P(('groups', 'loop'), 'width'), parts along dimension 0, may hold values from -6 to 6
- gate_weight: bfloat16 [8192, 14336], P('width', 'loop'), may hold values from -0.0625 to 0.0625
- up_weight: bfloat16 [8192, 14336], P('width', 'loop'), may hold values from -0.0625 to 0.0625
- down_weight: bfloat16 [14336, 8192], P('loop', 'width'), may hold values from -0.046875 to 0.046875
- out_grad: bfloat16 [384, 8192], P(('groups', 'loop'), 'width'), parts along dimension 0, may hold values from -6 to 6
Outputs:
- output: bfloat16 [384, 8192], P(('groups', 'loop'), 'width'), parts along dimension 0
- input_grad: bfloat16 [384, 8192], P(('groups', 'loop'), 'width'), parts along dimension 0
- gate_grad: bfloat16 [16384, 14336], P(('groups', 'width'), 'loop'), parts along dimension 0
- up_grad: bfloat16 [16384, 14336], P(('groups', 'width'), 'loop'), parts along dimension 0
- down_grad: bfloat16 [28672, 8192], P(('groups', 'loop'), 'width'), parts along dimension 0
The draws below stay inside these ranges and needn't reach their ends.
There are 2 independent parts, one for each index of `groups`. The reference program is written for one: setup_inputs(seed, part) draws one part's arguments, and reference() takes and returns one part's arrays. A program takes and returns all parts, laid end to end along the dimension named above; an argument that names none is the same for every part. Nothing has to cross between parts.
All inputs are finite; a program needn't handle non-finite values.
Results may differ from the reference program's by a relative error of at most 0.005.
Values may be sent and summed in bfloat16 or wider, within the bound.
No kernel may reach another device: no remote copies, remote signals or barrier semaphores. Data moves between devices by JAX's collectives and lax.ppermute only.
A program may use at most 192 MiB of HBM per device.

```python
import jax
import jax.numpy as jnp
from jax import lax

D = 8192
FF = 14336
TOKENS = 192


def steps_of(key, shape, cuts, smallest, top_value):
    gain, own = 1.0, jax.random.fold_in(key, 6)
    for dim, parts in cuts:
        draws = jnp.exp(jax.random.uniform(jax.random.fold_in(own, dim), (parts,), jnp.float32, smallest / len(cuts), top_value / len(cuts)))
        gain = gain * jnp.repeat(draws, shape[dim] // parts).reshape([-1 if axis == dim else 1 for axis in range(len(shape))])
    return gain


def gaussian(key, shape, spread, most, cuts=(), held_as=jnp.bfloat16):
    loudness = steps_of(key, shape, cuts, -0.22, 0.18) if cuts else 1.0
    result = jax.random.normal(key, shape, jnp.float32) * spread * loudness
    return jnp.minimum(jnp.maximum(result, -most), most).astype(held_as)


def setup_inputs(seed: int = 0, part: int = 0) -> dict:
    key_of = jax.random.split(jax.random.key(seed), 6)
    part_keys = jax.random.split(jax.random.fold_in(key_of[5], part), 6)
    inputs = gaussian(part_keys[0], (TOKENS, D), 1.0, 6.0, ((0, 4), (1, 4)))
    gate_weight = gaussian(key_of[1], (D, FF), D ** -0.5, 0.0625, ((0, 4), (1, 4)))
    up_weight = gaussian(key_of[2], (D, FF), D ** -0.5, 0.0625, ((0, 4), (1, 4)))
    down_weight = gaussian(key_of[3], (FF, D), FF ** -0.5, 0.046875, ((0, 4), (1, 4)))
    out_grad = gaussian(part_keys[4], (TOKENS, D), 1.0, 6.0, ((0, 4), (1, 4)))
    return dict(inputs=inputs, gate_weight=gate_weight, up_weight=up_weight, down_weight=down_weight, out_grad=out_grad)


def contract_rows(left, right):
    return lax.dot_general(left, right, (((0,), (0,)), ((), ())), preferred_element_type=jnp.float32)


def contract_cols(left, right):
    return lax.dot_general(left, right, (((1,), (1,)), ((), ())), preferred_element_type=jnp.float32)


def reference(inputs, gate_weight, up_weight, down_weight, out_grad):
    gate = jnp.dot(inputs, gate_weight, preferred_element_type=jnp.float32)
    up = jnp.dot(inputs, up_weight, preferred_element_type=jnp.float32)
    sig = jax.nn.sigmoid(gate)
    hidden = (gate * sig * up).astype(jnp.bfloat16)
    output = jnp.dot(hidden, down_weight, preferred_element_type=jnp.float32).astype(jnp.bfloat16)
    down_grad = contract_rows(hidden, out_grad).astype(jnp.bfloat16)
    hidden_grad = contract_cols(out_grad, down_weight)
    pre_gate = (hidden_grad * up * sig * (1.0 + gate * (1.0 - sig))).astype(jnp.bfloat16)
    pre_up = (hidden_grad * gate * sig).astype(jnp.bfloat16)
    input_grad = (contract_cols(pre_gate, gate_weight) + contract_cols(pre_up, up_weight)).astype(jnp.bfloat16)
    gate_grad = contract_rows(inputs, pre_gate).astype(jnp.bfloat16)
    up_grad = contract_rows(inputs, pre_up).astype(jnp.bfloat16)
    return output, input_grad, gate_grad, up_grad, down_grad
```

```python
import functools

import jax
import jax.numpy as jnp
from jax import lax
from jax.experimental import pallas as pl
from jax.experimental.pallas import tpu as pltpu
from jax.sharding import PartitionSpec as P

BF16 = jnp.bfloat16
F32 = jnp.float32
LANES = 128
VMEM = 40 * 1024 * 1024


def contract_rows(left, right):
    return lax.dot_general(left, right, (((0,), (0,)), ((), ())), preferred_element_type=F32)


def contract_cols(left, right):
    return lax.dot_general(left, right, (((1,), (1,)), ((), ())), preferred_element_type=F32)


def matmul(left, right):
    return jnp.dot(left, right, preferred_element_type=F32)


def block_of(size, most):
    return max(b for b in range(LANES, most + 1, LANES) if size % b == 0)


def ring_order(n):
    return [0] + list(range(1, n, 2)) + [k for k in range(n - 1, 1, -1) if k % 2 == 0]


def ring_perm(n):
    order = ring_order(n)
    return [(order[k], order[(k + 1) % n]) for k in range(n)]


def ring_place(index, n):
    order = ring_order(n)
    place = jnp.int32(0)
    for k in range(n):
        place = jnp.where(index == order[k], k, place)
    return place.astype(jnp.int32)


def ring_gather(own, axis, perm, n):
    slots = [own]
    for _ in range(n - 1):
        slots.append(lax.ppermute(slots[-1], axis, perm))
    return slots


def ring_scatter(slots, axis, perm, n):
    total = slots[1 % n]
    for h in range(1, n):
        got = lax.ppermute(total.astype(BF16), axis, perm)
        total = got.astype(F32) + slots[(h + 1) % n]
    return total


def together(*arrays):
    return lax.optimization_barrier(list(arrays))


def params():
    return pltpu.CompilerParams(vmem_limit_bytes=VMEM)


def cost(flops, moved):
    return pl.CostEstimate(flops=flops // 8, bytes_accessed=moved // 8, transcendentals=0)


def pre_body(places, rows, gate_w, up_w, gate, up, gate_sum, up_sum):
    k = pl.program_id(1)

    @pl.when(k == 0)
    def _():
        gate_sum[...] = jnp.zeros_like(gate_sum)
        up_sum[...] = jnp.zeros_like(up_sum)

    gate_sum[...] += matmul(rows[...], gate_w[...])
    up_sum[...] += matmul(rows[...], up_w[...])

    @pl.when(k == pl.num_programs(1) - 1)
    def _():
        gate[0] = gate_sum[...].astype(gate.dtype)
        up[0] = up_sum[...].astype(up.dtype)


def partial_pre(places, rows, gate_w, up_w, shard, dtype):
    count, (tokens, depth) = places.shape[0], rows.shape
    step = block_of(depth, 512)
    weight = pl.BlockSpec((step, shard), lambda j, k, p: (k, p[j]))
    result = pl.BlockSpec((1, tokens, shard), lambda j, k, p: (j, 0, 0))
    return pl.pallas_call(
        pre_body,
        grid_spec=pltpu.PrefetchScalarGridSpec(
            num_scalar_prefetch=1,
            grid=(count, depth // step),
            in_specs=[pl.BlockSpec((tokens, step), lambda j, k, p: (0, k)), weight, weight],
            out_specs=[result, result],
            scratch_shapes=[pltpu.VMEM((tokens, shard), F32)] * 2,
        ),
        out_shape=[jax.ShapeDtypeStruct((count, tokens, shard), dtype)] * 2,
        cost_estimate=cost(4 * count * tokens * depth * shard, 4 * count * depth * shard),
        compiler_params=params(),
        name="partial_pre",
    )(places, rows, gate_w, up_w)


def grad_body(places, rows, down_w, total):
    @pl.when(pl.program_id(1) == 0)
    def _():
        total[...] = jnp.zeros_like(total)

    total[0] += contract_cols(rows[...], down_w[...])


def partial_hidden_grad(places, rows, down_w, shard):
    count, (tokens, depth) = places.shape[0], rows.shape
    step = block_of(depth, 512)
    return pl.pallas_call(
        grad_body,
        grid_spec=pltpu.PrefetchScalarGridSpec(
            num_scalar_prefetch=1,
            grid=(count, depth // step),
            in_specs=[
                pl.BlockSpec((tokens, step), lambda j, k, p: (0, k)),
                pl.BlockSpec((shard, step), lambda j, k, p: (p[j], k)),
            ],
            out_specs=pl.BlockSpec((1, tokens, shard), lambda j, k, p: (j, 0, 0)),
        ),
        out_shape=jax.ShapeDtypeStruct((count, tokens, shard), F32),
        cost_estimate=cost(2 * count * tokens * depth * shard, 2 * count * depth * shard),
        compiler_params=params(),
        name="partial_hidden_grad",
    )(places, rows, down_w)


def down_body(first, place, hidden, down_w, rows, *rest):
    if first:
        total, grad = rest
        total[...] = matmul(hidden[...], down_w[...])
    else:
        before, _, total, grad = rest
        total[...] = before[...] + matmul(hidden[...], down_w[...])
    grad[...] = contract_rows(hidden[...], rows[...]).astype(BF16)


def down_shard(place, hidden, down_w, rows, before):
    tokens, shard = hidden.shape
    units, depth = down_w.shape
    step = block_of(depth, 512)
    first = before is None
    block = pl.BlockSpec((shard, step), lambda i, p: (p[0], i))
    part = pl.BlockSpec((tokens, step), lambda i, p: (0, i))
    anywhere = pl.BlockSpec(memory_space=pl.ANY)
    return pl.pallas_call(
        functools.partial(down_body, first),
        grid_spec=pltpu.PrefetchScalarGridSpec(
            num_scalar_prefetch=1,
            grid=(depth // step,),
            in_specs=[pl.BlockSpec((tokens, shard), lambda i, p: (0, 0)), block, part]
            + ([] if first else [part, anywhere]),
            out_specs=[part, block],
        ),
        out_shape=[
            jax.ShapeDtypeStruct((tokens, depth), F32),
            jax.ShapeDtypeStruct((units, depth), BF16),
        ],
        input_output_aliases={} if first else {4: 0, 5: 1},
        cost_estimate=cost(4 * tokens * depth * shard, 4 * depth * shard),
        compiler_params=params(),
        name="down_shard",
    )(place, hidden, down_w, rows, *([] if first else before))


def input_body(first, place, pre_gate, pre_up, gate_w, up_w, *rest):
    total = rest[-1]
    value = contract_cols(pre_gate[...], gate_w[...]) + contract_cols(pre_up[...], up_w[...])
    total[...] = value if first else rest[0][...] + value


def input_shard(place, pre_gate, pre_up, gate_w, up_w, before):
    tokens, shard = pre_gate.shape
    depth = gate_w.shape[0]
    step = block_of(depth, 256)
    first = before is None
    whole = pl.BlockSpec((tokens, shard), lambda i, p: (0, 0))
    block = pl.BlockSpec((step, shard), lambda i, p: (i, p[0]))
    part = pl.BlockSpec((tokens, step), lambda i, p: (0, i))
    return pl.pallas_call(
        functools.partial(input_body, first),
        grid_spec=pltpu.PrefetchScalarGridSpec(
            num_scalar_prefetch=1,
            grid=(depth // step,),
            in_specs=[whole, whole, block, block] + ([] if first else [part]),
            out_specs=part,
        ),
        out_shape=jax.ShapeDtypeStruct((tokens, depth), F32),
        input_output_aliases={} if first else {5: 0},
        cost_estimate=cost(4 * tokens * depth * shard, 4 * depth * shard),
        compiler_params=params(),
        name="input_shard",
    )(place, pre_gate, pre_up, gate_w, up_w, *([] if first else [before]))


def weight_body(place, pre_gate, pre_up, rows, *rest):
    gate_grad, up_grad = rest[-2:]
    gate_grad[...] = contract_rows(rows[...], pre_gate[...]).astype(BF16)
    up_grad[...] = contract_rows(rows[...], pre_up[...]).astype(BF16)


def weight_shard(place, pre_gate, pre_up, rows, units, before):
    tokens, shard = pre_gate.shape
    depth = rows.shape[1]
    step = block_of(depth, 256)
    first = before is None
    whole = pl.BlockSpec((tokens, shard), lambda i, p: (0, 0))
    block = pl.BlockSpec((step, shard), lambda i, p: (i, p[0]))
    part = pl.BlockSpec((tokens, step), lambda i, p: (0, i))
    anywhere = pl.BlockSpec(memory_space=pl.ANY)
    return pl.pallas_call(
        weight_body,
        grid_spec=pltpu.PrefetchScalarGridSpec(
            num_scalar_prefetch=1,
            grid=(depth // step,),
            in_specs=[whole, whole, part] + ([] if first else [anywhere, anywhere]),
            out_specs=[block, block],
        ),
        out_shape=[jax.ShapeDtypeStruct((depth, units), BF16)] * 2,
        input_output_aliases={} if first else {4: 0, 5: 1},
        cost_estimate=cost(4 * tokens * depth * shard, 4 * depth * shard),
        compiler_params=params(),
        name="weight_shard",
    )(place, pre_gate, pre_up, rows, *([] if first else before))


def shards(loop, width, inputs, gate_weight, up_weight, down_weight, out_grad):
    hidden_dev = gate_weight.shape[1]
    shard = hidden_dev // width
    chips = loop // 2
    own_rows = inputs.shape[0]

    z_perm = ring_perm(width)
    y_perm = [(2 * a + core, 2 * b + core) for a, b in ring_perm(chips) for core in (0, 1)]
    core_perm = [(k, k ^ 1) for k in range(loop)]

    def gather_core(mine):
        return jnp.concatenate(mine + [lax.ppermute(m, "loop", core_perm) for m in mine], axis=0)

    def scatter_loop(total):
        half = chips * own_rows
        mine = total[:half] + lax.ppermute(total[half:], "loop", core_perm)
        slots = [mine[k * own_rows : (k + 1) * own_rows] for k in range(chips)]
        return ring_scatter(slots, "loop", y_perm, chips).astype(BF16)

    place = ring_place(lax.axis_index("width"), width)
    places = lax.rem(place + width - jnp.arange(width, dtype=jnp.int32), jnp.int32(width))

    def hop(sent):
        return lax.ppermute(sent, "width", z_perm)

    def add(got, term):
        return got.astype(F32) + term

    mine = ring_gather(inputs, "loop", y_perm, chips)
    out_grad, mine[-1] = together(out_grad, mine[-1])
    gathered = gather_core(mine)
    gate_1, up_1 = partial_pre(places[1:2], gathered, gate_weight, up_weight, shard, BF16)
    rest, gate_1, up_1 = together(gathered, gate_1, up_1)
    order = jnp.concatenate([places[2:], places[:1]])
    gate_n, up_n = partial_pre(order, rest, gate_weight, up_weight, shard, F32)
    piece = gather_core(ring_gather(out_grad, "loop", y_perm, chips))
    grad_n = partial_hidden_grad(places, piece, down_weight, shard)

    gate, up, sent = hop(gate_1[0]), hop(up_1[0]), grad_n[1].astype(BF16)
    sent, gate_n, up_n = together(sent, gate_n, up_n)
    for h in range(1, width - 1):
        got = hop(sent)
        gate = hop(add(gate, gate_n[h - 1]).astype(BF16))
        up = hop(add(up, up_n[h - 1]).astype(BF16))
        sent = add(got, grad_n[h + 1]).astype(BF16)
    gate, up = add(gate, gate_n[width - 2]), add(up, up_n[width - 2])
    sig = jax.nn.sigmoid(gate)
    sent, hidden_own = together(sent, (gate * sig * up).astype(BF16))
    hidden_grad = add(hop(sent), grad_n[0])
    hidden = [hidden_own, hop(hidden_own)]

    down = list(down_shard(places[:1], hidden[0], down_weight, piece, None))
    pre_gate = [(hidden_grad * up * sig * (1.0 + gate * (1.0 - sig))).astype(BF16)]
    pre_up = [(hidden_grad * gate * sig).astype(BF16)]
    total, weights = None, None
    for k in range(width):
        here = places[k : k + 1]
        if k < width - 1:
            pre_gate.append(hop(pre_gate[k]))
            pre_up.append(hop(pre_up[k]))
        total = input_shard(here, pre_gate[k], pre_up[k], gate_weight, up_weight, total)
        weights = list(weight_shard(here, pre_gate[k], pre_up[k], gathered, hidden_dev, weights))
        if k < width - 1:
            if k < width - 2:
                hidden[k + 1], down[0] = together(hidden[k + 1], down[0])
                hidden.append(hop(hidden[k + 1]))
                pre_gate[k + 1], total = together(pre_gate[k + 1], total)
                pre_up[k + 1], weights[0] = together(pre_up[k + 1], weights[0])
            down = list(down_shard(places[k + 1 : k + 2], hidden[k + 1], down_weight, piece, down))
    output = scatter_loop(down[0])
    down_grad = down[1]
    input_grad = scatter_loop(total)
    gate_grad, up_grad = weights
    return (output, input_grad, gate_grad, up_grad, down_grad)


def plain(inputs, gate_weight, up_weight, down_weight, out_grad):
    gathered = lax.all_gather(inputs, "loop", axis=0, tiled=True)
    gate = lax.psum(matmul(gathered, gate_weight), "width")
    up = lax.psum(matmul(gathered, up_weight), "width")
    sig = jax.nn.sigmoid(gate)
    hidden = (gate * sig * up).astype(BF16)
    output = lax.psum_scatter(matmul(hidden, down_weight), "loop", scatter_dimension=0, tiled=True).astype(BF16)
    piece = lax.all_gather(out_grad, "loop", axis=0, tiled=True)
    down_grad = contract_rows(hidden, piece).astype(BF16)
    hidden_grad = lax.psum(contract_cols(piece, down_weight), "width")
    pre_gate = (hidden_grad * up * sig * (1.0 + gate * (1.0 - sig))).astype(BF16)
    pre_up = (hidden_grad * gate * sig).astype(BF16)
    input_grad = lax.psum_scatter(
        contract_cols(pre_gate, gate_weight) + contract_cols(pre_up, up_weight),
        "loop",
        scatter_dimension=0,
        tiled=True,
    ).astype(BF16)
    gate_grad = contract_rows(gathered, pre_gate).astype(BF16)
    up_grad = contract_rows(gathered, pre_up).astype(BF16)
    return (output, input_grad, gate_grad, up_grad, down_grad)


def solution(mesh):
    loop, width = mesh.shape["loop"], mesh.shape["width"]

    def layer(*arrays):
        units = arrays[1].shape[1]
        if units % (width * LANES) or loop % 2 or width < 2:
            return plain(*arrays)
        return shards(loop, width, *arrays)

    in_specs = (
        P(("groups", "loop"), "width"),
        P("width", "loop"),
        P("width", "loop"),
        P("loop", "width"),
        P(("groups", "loop"), "width"),
    )
    out_specs = (
        P(("groups", "loop"), "width"),
        P(("groups", "loop"), "width"),
        P(("groups", "width"), "loop"),
        P(("groups", "width"), "loop"),
        P(("groups", "loop"), "width"),
    )
    return jax.shard_map(layer, mesh=mesh, in_specs=in_specs, out_specs=out_specs, check_vma=False)
```

```python
import functools

import jax
import jax.numpy as jnp
from jax import lax
from jax.experimental import pallas as pl
from jax.experimental.pallas import tpu as pltpu
from jax.sharding import PartitionSpec as P

BF16 = jnp.bfloat16
F32 = jnp.float32
LANES = 128
VMEM = 48 * 1024 * 1024


def contract_rows(left, right):
    return lax.dot_general(left, right, (((0,), (0,)), ((), ())), preferred_element_type=F32)


def contract_cols(left, right):
    return lax.dot_general(left, right, (((1,), (1,)), ((), ())), preferred_element_type=F32)


def matmul(left, right):
    return jnp.dot(left, right, preferred_element_type=F32)


def block_of(size, most):
    return max(b for b in range(LANES, most + 1, LANES) if size % b == 0)


def ring_order(n):
    return [0] + list(range(1, n, 2)) + [k for k in range(n - 1, 1, -1) if k % 2 == 0]


def ring_perm(n):
    order = ring_order(n)
    return [(order[k], order[(k + 1) % n]) for k in range(n)]


def ring_place(index, n):
    order = ring_order(n)
    place = jnp.int32(0)
    for k in range(n):
        place = jnp.where(index == order[k], k, place)
    return place.astype(jnp.int32)


def ring_gather(own, axis, perm, n):
    slots = [own]
    for _ in range(n - 1):
        slots.append(lax.ppermute(slots[-1], axis, perm))
    return slots


def ring_scatter(slots, axis, perm, n):
    total = slots[1 % n]
    for h in range(1, n):
        got = lax.ppermute(total.astype(BF16), axis, perm)
        total = got.astype(F32) + slots[(h + 1) % n]
    return total


def together(*arrays):
    return lax.optimization_barrier(list(arrays))


def params():
    return pltpu.CompilerParams(vmem_limit_bytes=VMEM)


def cost(flops, moved):
    return pl.CostEstimate(flops=flops // 8, bytes_accessed=moved // 8, transcendentals=0)


def whole():
    return pl.BlockSpec(memory_space=pltpu.VMEM)


def anywhere():
    return pl.BlockSpec(memory_space=pl.ANY)


def number():
    return pl.BlockSpec(memory_space=pltpu.SMEM)


def copies(blocks, held, sems):
    return [pltpu.make_async_copy(block, held.at[k], sems.at[k]) for k, block in enumerate(blocks)]


def start(*lists):
    for group in zip(*lists):
        for copy in group:
            copy.start()


def columns_of(place, shard):
    return pl.ds(pl.multiple_of(place * shard, LANES), shard)


def pre_body(parts, place, rows, gate_w, up_w, gate, up, gate_held, up_held, gate_sum, up_sum, sems):
    depth, shard = gate_held.shape[1:]
    columns = columns_of(place[0], shard)
    here = [pl.ds(k * depth, depth) for k in range(parts)]
    gate_in = copies([gate_w.at[h, columns] for h in here], gate_held, sems.at[0])
    up_in = copies([up_w.at[h, columns] for h in here], up_held, sems.at[1])
    start(gate_in, up_in)
    for k in range(parts):
        part = rows[:, k * depth : (k + 1) * depth]
        for copy, held, total, out in (
            (gate_in[k], gate_held, gate_sum, gate),
            (up_in[k], up_held, up_sum, up),
        ):
            copy.wait()
            value = matmul(part, held[k])
            if k:
                value += total[...]
            if k < parts - 1:
                total[...] = value
            else:
                out[...] = value.astype(out.dtype)


def partial_pre(place, rows, gate_w, up_w, shard, dtype):
    tokens, depth = rows.shape
    parts = depth // block_of(depth, 512)
    held = pltpu.VMEM((parts, depth // parts, shard), BF16)
    return pl.pallas_call(
        functools.partial(pre_body, parts),
        in_specs=[number(), whole(), anywhere(), anywhere()],
        out_specs=[whole()] * 2,
        out_shape=[jax.ShapeDtypeStruct((tokens, shard), dtype)] * 2,
        scratch_shapes=[held, held]
        + [pltpu.VMEM((tokens, shard), F32)] * 2
        + [pltpu.SemaphoreType.DMA((2, parts))],
        cost_estimate=cost(4 * tokens * depth * shard, 4 * depth * shard),
        compiler_params=params(),
        name="partial_pre",
    )(place, rows, gate_w, up_w)


def grad_body(count, places, rows_t, down_w, total, held, sems):
    shard = held.shape[1]
    loads = copies(
        [down_w.at[pl.ds(pl.multiple_of(places[j] * shard, LANES), shard)] for j in range(count)], held, sems
    )
    start(loads)
    for j in range(count):
        loads[j].wait()
        total[j] = matmul(held[j], rows_t[...]).T


def partial_hidden_grad(places, rows_t, down_w, shard):
    count, (depth, tokens) = places.shape[0], rows_t.shape
    return pl.pallas_call(
        functools.partial(grad_body, count),
        in_specs=[number(), whole(), anywhere()],
        out_specs=whole(),
        out_shape=jax.ShapeDtypeStruct((count, tokens, shard), F32),
        scratch_shapes=[pltpu.VMEM((count, shard, depth), BF16), pltpu.SemaphoreType.DMA((count,))],
        cost_estimate=cost(2 * count * tokens * depth * shard, 2 * count * depth * shard),
        compiler_params=params(),
        name="partial_hidden_grad",
    )(places, rows_t, down_w)


def down_body(parts, first, place, hidden, down_w, rows, *rest):
    total, grad, held, made, hidden_t, in_sems, out_sems = rest[-7:]
    shard, step = held.shape[1:]
    units = columns_of(place[0], shard)
    here = [pl.ds(k * step, step) for k in range(parts)]
    loads = copies([down_w.at[units, h] for h in here], held, in_sems)
    start(loads)
    hidden_t[...] = hidden[...].T
    stores = []
    for k in range(parts):
        span = slice(k * step, (k + 1) * step)
        made[k] = matmul(hidden_t[...], rows[:, span]).astype(BF16)
        stores.append(pltpu.make_async_copy(made.at[k], grad.at[units, here[k]], out_sems.at[k]))
        stores[k].start()
        loads[k].wait()
        value = matmul(hidden[...], held[k])
        total[:, span] = value if first else rest[0][:, span] + value
    for store in stores:
        store.wait()


def down_shard(place, hidden, down_w, rows, before):
    tokens, shard = hidden.shape
    units, depth = down_w.shape
    step = block_of(depth, 512)
    parts = depth // step
    first = before is None
    held = pltpu.VMEM((parts, shard, step), BF16)
    return list(
        pl.pallas_call(
            functools.partial(down_body, parts, first),
            in_specs=[number(), whole(), anywhere(), whole()] + ([] if first else [whole(), anywhere()]),
            out_specs=[whole(), anywhere()],
            out_shape=[
                jax.ShapeDtypeStruct((tokens, depth), F32),
                jax.ShapeDtypeStruct((units, depth), BF16),
            ],
            scratch_shapes=[held, held, pltpu.VMEM((shard, tokens), BF16)] + [pltpu.SemaphoreType.DMA((parts,))] * 2,
            input_output_aliases={} if first else {4: 0, 5: 1},
            cost_estimate=cost(4 * tokens * depth * shard, 4 * depth * shard),
            compiler_params=params(),
            name="down_shard",
        )(place, hidden, down_w, rows, *([] if first else before))
    )


def input_body(parts, first, place, pre_gate, pre_up, gate_w, up_w, *rest):
    total, gate_held, up_held, gate_t, up_t, sems = rest[-6:]
    step, shard = gate_held.shape[1:]
    columns = columns_of(place[0], shard)
    here = [pl.ds(k * step, step) for k in range(parts)]
    gate_in = copies([gate_w.at[h, columns] for h in here], gate_held, sems.at[0])
    up_in = copies([up_w.at[h, columns] for h in here], up_held, sems.at[1])
    start(gate_in, up_in)
    gate_t[...] = pre_gate[...].T
    up_t[...] = pre_up[...].T
    for k in range(parts):
        span = slice(k * step, (k + 1) * step)
        gate_in[k].wait()
        value = matmul(gate_held[k], gate_t[...])
        up_in[k].wait()
        value = (value + matmul(up_held[k], up_t[...])).T
        total[:, span] = value if first else rest[0][:, span] + value


def input_shard(place, pre_gate, pre_up, gate_w, up_w, before):
    tokens, shard = pre_gate.shape
    depth = gate_w.shape[0]
    step = block_of(depth, 256)
    parts = depth // step
    first = before is None
    held = pltpu.VMEM((parts, step, shard), BF16)
    turned = pltpu.VMEM((shard, tokens), BF16)
    return pl.pallas_call(
        functools.partial(input_body, parts, first),
        in_specs=[number(), whole(), whole(), anywhere(), anywhere()] + ([] if first else [whole()]),
        out_specs=whole(),
        out_shape=jax.ShapeDtypeStruct((tokens, depth), F32),
        scratch_shapes=[held, held, turned, turned, pltpu.SemaphoreType.DMA((2, parts))],
        input_output_aliases={} if first else {5: 0},
        cost_estimate=cost(4 * tokens * depth * shard, 4 * depth * shard),
        compiler_params=params(),
        name="input_shard",
    )(place, pre_gate, pre_up, gate_w, up_w, *([] if first else [before]))


def weight_body(parts, place, pre_gate, pre_up, rows_t, *rest):
    gate_grad, up_grad, gate_made, up_made, sems = rest[-5:]
    step, shard = gate_made.shape[1:]
    columns = columns_of(place[0], shard)
    stores = []
    for k in range(parts):
        here = pl.ds(k * step, step)
        rows = rows_t[k * step : (k + 1) * step]
        for n, (pre, made, grad) in enumerate(((pre_gate, gate_made, gate_grad), (pre_up, up_made, up_grad))):
            made[k] = matmul(rows, pre[...]).astype(BF16)
            stores.append(pltpu.make_async_copy(made.at[k], grad.at[here, columns], sems.at[n, k]))
            stores[-1].start()
    for store in stores:
        store.wait()


def weight_shard(place, pre_gate, pre_up, rows_t, units, before):
    tokens, shard = pre_gate.shape
    depth = rows_t.shape[0]
    step = block_of(depth, 256)
    parts = depth // step
    first = before is None
    made = pltpu.VMEM((parts, step, shard), BF16)
    return list(
        pl.pallas_call(
            functools.partial(weight_body, parts),
            in_specs=[number(), whole(), whole(), whole()] + ([] if first else [anywhere()] * 2),
            out_specs=[anywhere()] * 2,
            out_shape=[jax.ShapeDtypeStruct((depth, units), BF16)] * 2,
            scratch_shapes=[made, made, pltpu.SemaphoreType.DMA((2, parts))],
            input_output_aliases={} if first else {4: 0, 5: 1},
            cost_estimate=cost(4 * tokens * depth * shard, 4 * depth * shard),
            compiler_params=params(),
            name="weight_shard",
        )(place, pre_gate, pre_up, rows_t, *([] if first else before))
    )


def shards(loop, width, inputs, gate_weight, up_weight, down_weight, out_grad):
    hidden_dev = gate_weight.shape[1]
    shard = hidden_dev // width
    chips = loop // 2
    own_rows = inputs.shape[0]

    z_perm = ring_perm(width)
    y_perm = [(2 * a + core, 2 * b + core) for a, b in ring_perm(chips) for core in (0, 1)]
    core_perm = [(k, k ^ 1) for k in range(loop)]

    def gather_core(mine):
        return jnp.concatenate(mine + [lax.ppermute(m, "loop", core_perm) for m in mine], axis=0)

    def scatter_loop(total):
        half = chips * own_rows
        mine = total[:half] + lax.ppermute(total[half:], "loop", core_perm)
        slots = [mine[k * own_rows : (k + 1) * own_rows] for k in range(chips)]
        return ring_scatter(slots, "loop", y_perm, chips).astype(BF16)

    place = ring_place(lax.axis_index("width"), width)
    places = lax.rem(place + width - jnp.arange(width, dtype=jnp.int32), jnp.int32(width))

    def hop(sent):
        return lax.ppermute(sent, "width", z_perm)

    def add(got, term):
        return got.astype(F32) + term

    mine = ring_gather(inputs, "loop", y_perm, chips)
    out_grad, mine[-1] = together(out_grad, mine[-1])
    gathered = gather_core(mine)
    def pre_of(slot, rows, dtype=F32):
        return partial_pre(places[slot : slot + 1], rows, gate_weight, up_weight, shard, dtype)

    slots = [(k + 1) % width for k in range(width)]
    terms = {1: pre_of(1, gathered, BF16)}
    gate, up = hop(terms[1][0]), hop(terms[1][1])
    rows, *terms[1] = together(gathered, *terms[1])
    terms[slots[1]] = pre_of(slots[1], rows)
    piece = gather_core(ring_gather(out_grad, "loop", y_perm, chips))
    piece_t, *terms[slots[1]] = together(piece.T, *terms[slots[1]])
    grad_n = partial_hidden_grad(places, piece_t, down_weight, shard)
    rows, grad_n = together(rows, grad_n)
    for slot in slots[2:]:
        terms[slot] = pre_of(slot, rows)

    sent = grad_n[1].astype(BF16)
    for h in range(1, width - 1):
        got = hop(sent)
        term = terms[slots[h]]
        gate, up = hop(add(gate, term[0]).astype(BF16)), hop(add(up, term[1]).astype(BF16))
        sent = add(got, grad_n[h + 1]).astype(BF16)
    gate, up = add(gate, terms[0][0]), add(up, terms[0][1])
    sig = jax.nn.sigmoid(gate)
    sent, hidden_own = together(sent, (gate * sig * up).astype(BF16))
    hidden_grad = add(hop(sent), grad_n[0])
    hidden = [hidden_own, hop(hidden_own)]

    rows_t = gathered.T
    down = down_shard(places[:1], hidden[0], down_weight, piece, None)
    pre_gate = [(hidden_grad * up * sig * (1.0 + gate * (1.0 - sig))).astype(BF16)]
    pre_up = [(hidden_grad * gate * sig).astype(BF16)]
    total, grads = None, None
    for k in range(width):
        here = places[k : k + 1]
        if k < width - 1:
            pre_gate.append(hop(pre_gate[k]))
            pre_up.append(hop(pre_up[k]))
        total = input_shard(here, pre_gate[k], pre_up[k], gate_weight, up_weight, total)
        grads = weight_shard(here, pre_gate[k], pre_up[k], rows_t, hidden_dev, grads)
        if k < width - 1:
            if k < width - 2:
                hidden[k + 1], down[0] = together(hidden[k + 1], down[0])
                hidden.append(hop(hidden[k + 1]))
                pre_gate[k + 1], total = together(pre_gate[k + 1], total)
                pre_up[k + 1], grads[0] = together(pre_up[k + 1], grads[0])
            down = down_shard(places[k + 1 : k + 2], hidden[k + 1], down_weight, piece, down)
    output = scatter_loop(down[0])
    down_grad = down[1]
    input_grad = scatter_loop(total)
    gate_grad, up_grad = grads
    return (output, input_grad, gate_grad, up_grad, down_grad)


def plain(inputs, gate_weight, up_weight, down_weight, out_grad):
    gathered = lax.all_gather(inputs, "loop", axis=0, tiled=True)
    gate = lax.psum(matmul(gathered, gate_weight), "width")
    up = lax.psum(matmul(gathered, up_weight), "width")
    sig = jax.nn.sigmoid(gate)
    hidden = (gate * sig * up).astype(BF16)
    output = lax.psum_scatter(matmul(hidden, down_weight), "loop", scatter_dimension=0, tiled=True).astype(BF16)
    piece = lax.all_gather(out_grad, "loop", axis=0, tiled=True)
    down_grad = contract_rows(hidden, piece).astype(BF16)
    hidden_grad = lax.psum(contract_cols(piece, down_weight), "width")
    pre_gate = (hidden_grad * up * sig * (1.0 + gate * (1.0 - sig))).astype(BF16)
    pre_up = (hidden_grad * gate * sig).astype(BF16)
    input_grad = lax.psum_scatter(
        contract_cols(pre_gate, gate_weight) + contract_cols(pre_up, up_weight),
        "loop",
        scatter_dimension=0,
        tiled=True,
    ).astype(BF16)
    gate_grad = contract_rows(gathered, pre_gate).astype(BF16)
    up_grad = contract_rows(gathered, pre_up).astype(BF16)
    return (output, input_grad, gate_grad, up_grad, down_grad)


def solution(mesh):
    loop, width = mesh.shape["loop"], mesh.shape["width"]

    def layer(*arrays):
        units = arrays[1].shape[1]
        if units % (width * LANES) or loop % 2 or width < 2:
            return plain(*arrays)
        return shards(loop, width, *arrays)

    in_specs = (
        P(("groups", "loop"), "width"),
        P("width", "loop"),
        P("width", "loop"),
        P("loop", "width"),
        P(("groups", "loop"), "width"),
    )
    out_specs = (
        P(("groups", "loop"), "width"),
        P(("groups", "loop"), "width"),
        P(("groups", "width"), "loop"),
        P(("groups", "width"), "loop"),
        P(("groups", "loop"), "width"),
    )
    return jax.shard_map(layer, mesh=mesh, in_specs=in_specs, out_specs=out_specs, check_vma=False)
```

```python
import functools

import jax
import jax.numpy as jnp
from jax import lax
from jax.experimental import pallas as pl
from jax.experimental.pallas import tpu as pltpu
from jax.sharding import PartitionSpec as P

BF16 = jnp.bfloat16
F32 = jnp.float32
LANES = 128
MIB = 1024 * 1024
KERNEL_VMEM = 46 * MIB


def contract_rows(left, right):
    return lax.dot_general(left, right, (((0,), (0,)), ((), ())), preferred_element_type=F32)


def contract_cols(left, right):
    return lax.dot_general(left, right, (((1,), (1,)), ((), ())), preferred_element_type=F32)


def matmul(left, right):
    return jnp.dot(left, right, preferred_element_type=F32)


def block_of(size, most):
    return max(b for b in range(LANES, most + 1, LANES) if size % b == 0)


def ring_order(n):
    return [0] + list(range(1, n, 2)) + [k for k in range(n - 1, 1, -1) if k % 2 == 0]


def ring_perm(n):
    order = ring_order(n)
    return [(order[k], order[(k + 1) % n]) for k in range(n)]


def ring_place(index, n):
    order = ring_order(n)
    place = jnp.int32(0)
    for k in range(n):
        place = jnp.where(index == order[k], k, place)
    return place.astype(jnp.int32)


def ring_gather(own, axis, perm, n):
    slots = [own]
    for _ in range(n - 1):
        slots.append(lax.ppermute(slots[-1], axis, perm))
    return slots


def ring_scatter(slots, axis, perm, n):
    total = slots[1 % n]
    for h in range(1, n):
        got = lax.ppermute(total.astype(BF16), axis, perm)
        total = got.astype(F32) + slots[(h + 1) % n]
    return total


def together(*arrays):
    return lax.optimization_barrier(list(arrays))


def params():
    return pltpu.CompilerParams(vmem_limit_bytes=KERNEL_VMEM)


def cost(flops, moved):
    return pl.CostEstimate(flops=flops // 64, bytes_accessed=moved // 64, transcendentals=0)


def whole():
    return pl.BlockSpec(memory_space=pltpu.VMEM)


def in_hbm():
    return pl.BlockSpec(memory_space=pltpu.HBM)


def number():
    return pl.BlockSpec(memory_space=pltpu.SMEM)


def copies(blocks, held, sems):
    return [pltpu.make_async_copy(block, held.at[k], sems.at[k]) for k, block in enumerate(blocks)]


def start(*lists):
    for group in zip(*lists):
        for copy in group:
            copy.start()


def columns_of(place, shard):
    return pl.ds(pl.multiple_of(place * shard, LANES), shard)


def load_body(parts, place, gate_w, up_w, gate_held, up_held, sems):
    depth, shard = gate_held.shape
    step, columns = depth // parts, columns_of(place[0], shard)
    loads = []
    for n, (source, held) in enumerate(((gate_w, gate_held), (up_w, up_held))):
        for k in range(parts):
            here = pl.ds(k * step, step)
            loads.append(pltpu.make_async_copy(source.at[here, columns], held.at[here], sems.at[n, k]))
            loads[-1].start()
    for copy in loads:
        copy.wait()


def load(place, gate_w, up_w, shard):
    parts, depth = 4, gate_w.shape[0]
    return pl.pallas_call(
        functools.partial(load_body, parts),
        in_specs=[number(), in_hbm(), in_hbm()],
        out_specs=[whole()] * 2,
        out_shape=[jax.ShapeDtypeStruct((depth, shard), gate_w.dtype)] * 2,
        scratch_shapes=[pltpu.SemaphoreType.DMA((2, parts))],
        cost_estimate=cost(0, 4 * depth * shard),
        compiler_params=params(),
        name="load",
    )(place, gate_w, up_w)


def pre_body(parts, place, rows, gate_w, up_w, gate, up, gate_held, up_held, gate_sum, up_sum, sems):
    depth, shard = gate_held.shape[1:]
    columns = columns_of(place[0], shard)
    here = [pl.ds(k * depth, depth) for k in range(parts)]
    gate_in = copies([gate_w.at[h, columns] for h in here], gate_held, sems.at[0])
    up_in = copies([up_w.at[h, columns] for h in here], up_held, sems.at[1])
    start(gate_in, up_in)
    for k in range(parts):
        part = rows[:, k * depth : (k + 1) * depth]
        for copy, held, total, out in (
            (gate_in[k], gate_held, gate_sum, gate),
            (up_in[k], up_held, up_sum, up),
        ):
            copy.wait()
            value = matmul(part, held[k])
            if k:
                value += total[...]
            if k < parts - 1:
                total[...] = value
            else:
                out[...] = value.astype(out.dtype)


def partial_pre(place, rows, gate_w, up_w, shard, dtype):
    tokens, depth = rows.shape
    parts = depth // block_of(depth, 512)
    held = pltpu.VMEM((parts, depth // parts, shard), BF16)
    return pl.pallas_call(
        functools.partial(pre_body, parts),
        in_specs=[number(), whole(), in_hbm(), in_hbm()],
        out_specs=[whole()] * 2,
        out_shape=[jax.ShapeDtypeStruct((tokens, shard), dtype)] * 2,
        scratch_shapes=[held, held]
        + [pltpu.VMEM((tokens, shard), F32)] * 2
        + [pltpu.SemaphoreType.DMA((2, parts))],
        cost_estimate=cost(4 * tokens * depth * shard, 4 * depth * shard),
        compiler_params=params(),
        name="partial_pre",
    )(place, rows, gate_w, up_w)


def grad_body(count, places, rows, down_w, total, held, rows_t, sems):
    shard = held.shape[1]
    loads = copies(
        [down_w.at[pl.ds(pl.multiple_of(places[j] * shard, LANES), shard)] for j in range(count)], held, sems
    )
    start(loads)
    rows_t[...] = rows[...].T
    half = shard // 2
    for j in range(count):
        loads[j].wait()
        low, high = matmul(held[j, :half], rows_t[...]), matmul(held[j, half:], rows_t[...])
        total[j] = jnp.concatenate([low, high], axis=0).T


def partial_hidden_grad(places, rows, down_w, shard):
    count, (tokens, depth) = places.shape[0], rows.shape
    return pl.pallas_call(
        functools.partial(grad_body, count),
        in_specs=[number(), whole(), in_hbm()],
        out_specs=whole(),
        out_shape=jax.ShapeDtypeStruct((count, tokens, shard), F32),
        scratch_shapes=[
            pltpu.VMEM((count, shard, depth), BF16),
            pltpu.VMEM((depth, tokens), BF16),
            pltpu.SemaphoreType.DMA((count,)),
        ],
        cost_estimate=cost(2 * count * tokens * depth * shard, 2 * count * depth * shard),
        compiler_params=params(),
        name="partial_hidden_grad",
    )(places, rows, down_w)


def down_body(parts, first, place, hidden, down_w, rows, *rest):
    total, grad, held, made, hidden_t, in_sems, out_sems = rest[-7:]
    shard, step = held.shape[1:]
    units = columns_of(place[0], shard)
    here = [pl.ds(k * step, step) for k in range(parts)]
    loads = copies([down_w.at[units, h] for h in here], held, in_sems)
    start(loads)
    hidden_t[...] = hidden[...].T
    stores = []
    for k in range(parts):
        span = slice(k * step, (k + 1) * step)
        made[k] = matmul(hidden_t[...], rows[:, span]).astype(BF16)
        stores.append(pltpu.make_async_copy(made.at[k], grad.at[units, here[k]], out_sems.at[k]))
        stores[k].start()
        loads[k].wait()
        value = matmul(hidden[...], held[k])
        total[:, span] = value if first else rest[0][:, span] + value
    for store in stores:
        store.wait()


def down_shard(place, hidden, down_w, rows, before):
    tokens, shard = hidden.shape
    units, depth = down_w.shape
    step = block_of(depth, 512)
    parts = depth // step
    first = before is None
    held = pltpu.VMEM((parts, shard, step), BF16)
    return list(
        pl.pallas_call(
            functools.partial(down_body, parts, first),
            in_specs=[number(), whole(), in_hbm(), whole()] + ([] if first else [whole(), in_hbm()]),
            out_specs=[whole(), in_hbm()],
            out_shape=[
                jax.ShapeDtypeStruct((tokens, depth), F32),
                jax.ShapeDtypeStruct((units, depth), BF16),
            ],
            scratch_shapes=[held, held, pltpu.VMEM((shard, tokens), BF16)] + [pltpu.SemaphoreType.DMA((parts,))] * 2,
            input_output_aliases={} if first else {4: 0, 5: 1},
            cost_estimate=cost(4 * tokens * depth * shard, 4 * depth * shard),
            compiler_params=params(),
            name="down_shard",
        )(place, hidden, down_w, rows, *([] if first else before))
    )


def turn_body(source, out):
    out[...] = source[...].T


def turn(source):
    rows, cols = source.shape
    return pl.pallas_call(
        turn_body,
        in_specs=[whole()],
        out_specs=whole(),
        out_shape=jax.ShapeDtypeStruct((cols, rows), source.dtype),
        cost_estimate=cost(0, 4 * source.size),
        compiler_params=params(),
        name="turn",
    )(source)


def weight_body(parts, place, pre, rows_t, *rest):
    grad, made, sems = rest[-3:]
    step, shard = made.shape[1:]
    columns = columns_of(place[0], shard)
    stores = []
    for k in range(parts):
        made[k] = matmul(rows_t[k * step : (k + 1) * step], pre[...]).astype(BF16)
        stores.append(pltpu.make_async_copy(made.at[k], grad.at[pl.ds(k * step, step), columns], sems.at[k]))
        stores[k].start()
    for store in stores:
        store.wait()


def weight_shard(place, pre, rows_t, units, before):
    tokens, shard = pre.shape
    depth = rows_t.shape[0]
    step = block_of(depth, 512)
    parts = depth // step
    first = before is None
    return pl.pallas_call(
        functools.partial(weight_body, parts),
        in_specs=[number(), whole(), whole()] + ([] if first else [in_hbm()]),
        out_specs=in_hbm(),
        out_shape=jax.ShapeDtypeStruct((depth, units), BF16),
        scratch_shapes=[pltpu.VMEM((parts, step, shard), BF16), pltpu.SemaphoreType.DMA((parts,))],
        input_output_aliases={} if first else {3: 0},
        cost_estimate=cost(2 * tokens * depth * shard, 2 * depth * shard),
        compiler_params=params(),
        name="weight_shard",
    )(place, pre, rows_t, *([] if first else [before]))


def shards(loop, width, inputs, gate_weight, up_weight, down_weight, out_grad):
    hidden_dev = gate_weight.shape[1]
    shard = hidden_dev // width
    chips = loop // 2
    own_rows = inputs.shape[0]

    z_perm = ring_perm(width)
    y_perm = [(2 * a + core, 2 * b + core) for a, b in ring_perm(chips) for core in (0, 1)]
    core_perm = [(k, k ^ 1) for k in range(loop)]

    def gather_core(mine):
        return jnp.concatenate(mine + [lax.ppermute(m, "loop", core_perm) for m in mine], axis=0)

    def scatter_chips(mine):
        slots = [mine[k * own_rows : (k + 1) * own_rows] for k in range(chips)]
        return ring_scatter(slots, "loop", y_perm, chips).astype(BF16)

    def scatter_loop(total):
        half = chips * own_rows
        return scatter_chips(total[:half] + lax.ppermute(total[half:], "loop", core_perm))

    place = ring_place(lax.axis_index("width"), width)
    places = lax.rem(place + width - jnp.arange(width, dtype=jnp.int32), jnp.int32(width))

    def hop(sent):
        return lax.ppermute(sent, "width", z_perm)

    def add(got, term):
        return got.astype(F32) + term

    def slot_of(array, slot):
        return lax.dynamic_slice_in_dim(array, places[slot] * shard, shard, axis=1)

    def pre_of(slot, rows):
        return partial_pre(places[slot : slot + 1], rows, gate_weight, up_weight, shard, F32)

    gate_held, up_held = load(places[1:2], gate_weight, up_weight, shard)
    mine = ring_gather(inputs, "loop", y_perm, chips)
    out_grad, mine[-1] = together(out_grad, mine[-1])
    gathered = gather_core(mine)
    gate_first, up_first = matmul(gathered, gate_held).astype(BF16), matmul(gathered, up_held).astype(BF16)
    gate, up = hop(gate_first), hop(up_first)
    rows, gate_first, up_first = together(gathered, gate_first, up_first)
    slots = [(k + 1) % width for k in range(width)]
    terms = [None] * width
    terms[slots[1]] = pre_of(slots[1], rows)
    piece = gather_core(ring_gather(out_grad, "loop", y_perm, chips))
    piece, *terms[slots[1]] = together(piece, *terms[slots[1]])
    grad_n = partial_hidden_grad(places, piece, down_weight, shard)
    rows, grad_n = together(rows, grad_n)
    for slot in slots[2:]:
        terms[slot] = pre_of(slot, rows)

    sent = grad_n[1].astype(BF16)
    for h in range(1, width - 1):
        got = hop(sent)
        gate = hop(add(gate, terms[slots[h]][0]).astype(BF16))
        up = hop(add(up, terms[slots[h]][1]).astype(BF16))
        sent = add(got, grad_n[h + 1]).astype(BF16)
    gate, up = add(gate, terms[0][0]), add(up, terms[0][1])
    sig = jax.nn.sigmoid(gate)
    sent, hidden_own = together(sent, (gate * sig * up).astype(BF16))
    hidden_grad = add(hop(sent), grad_n[0])
    hidden = [hidden_own, hop(hidden_own)]

    rows_t = turn(gathered)
    down = down_shard(places[:1], hidden[0], down_weight, piece, None)
    pre_gate = [(hidden_grad * up * sig * (1.0 + gate * (1.0 - sig))).astype(BF16)]
    pre_up = [(hidden_grad * gate * sig).astype(BF16)]
    total, gate_grad, up_grad = 0.0, None, None
    for k in range(width):
        here, last = places[k : k + 1], k == width - 1
        if not last:
            pre_gate.append(hop(pre_gate[k]))
            pre_up.append(hop(pre_up[k]))
        if last:
            output = scatter_loop(down[0])
            arrays = pre_gate[k], pre_up[k], gate_grad, up_grad, output
            pre_gate[k], pre_up[k], gate_grad, up_grad, output = together(*arrays)
        total = total + (
            contract_cols(pre_gate[k], slot_of(gate_weight, k)) + contract_cols(pre_up[k], slot_of(up_weight, k))
        )
        if last:
            break
        gate_grad = weight_shard(here, pre_gate[k], rows_t, hidden_dev, gate_grad)
        up_grad = weight_shard(here, pre_up[k], rows_t, hidden_dev, up_grad)
        if k < width - 2:
            hidden[k + 1], down[0] = together(hidden[k + 1], down[0])
            hidden.append(hop(hidden[k + 1]))
            pre_gate[k + 1], total = together(pre_gate[k + 1], total)
            pre_up[k + 1], gate_grad, up_grad = together(pre_up[k + 1], gate_grad, up_grad)
        down = down_shard(places[k + 1 : k + 2], hidden[k + 1], down_weight, piece, down)
    other = lax.ppermute(total[chips * own_rows :], "loop", core_perm)
    pre_last, total = together(pre_gate[-1], total)
    gate_grad = weight_shard(here, pre_last, rows_t, hidden_dev, gate_grad)
    other, gate_grad = together(other, gate_grad)
    input_grad = scatter_chips(total[: chips * own_rows] + other)
    up_grad = weight_shard(here, pre_up[-1], rows_t, hidden_dev, up_grad)
    down_grad = down[1]
    return (output, input_grad, gate_grad, up_grad, down_grad)


def plain(inputs, gate_weight, up_weight, down_weight, out_grad):
    gathered = lax.all_gather(inputs, "loop", axis=0, tiled=True)
    gate = lax.psum(matmul(gathered, gate_weight), "width")
    up = lax.psum(matmul(gathered, up_weight), "width")
    sig = jax.nn.sigmoid(gate)
    hidden = (gate * sig * up).astype(BF16)
    output = lax.psum_scatter(matmul(hidden, down_weight), "loop", scatter_dimension=0, tiled=True).astype(BF16)
    piece = lax.all_gather(out_grad, "loop", axis=0, tiled=True)
    down_grad = contract_rows(hidden, piece).astype(BF16)
    hidden_grad = lax.psum(contract_cols(piece, down_weight), "width")
    pre_gate = (hidden_grad * up * sig * (1.0 + gate * (1.0 - sig))).astype(BF16)
    pre_up = (hidden_grad * gate * sig).astype(BF16)
    input_grad = lax.psum_scatter(
        contract_cols(pre_gate, gate_weight) + contract_cols(pre_up, up_weight),
        "loop",
        scatter_dimension=0,
        tiled=True,
    ).astype(BF16)
    gate_grad = contract_rows(gathered, pre_gate).astype(BF16)
    up_grad = contract_rows(gathered, pre_up).astype(BF16)
    return (output, input_grad, gate_grad, up_grad, down_grad)


def solution(mesh):
    loop, width = mesh.shape["loop"], mesh.shape["width"]

    def layer(*arrays):
        units = arrays[1].shape[1]
        if units % (width * LANES) or loop % 2 or width < 2:
            return plain(*arrays)
        return shards(loop, width, *arrays)

    in_specs = (
        P(("groups", "loop"), "width"),
        P("width", "loop"),
        P("width", "loop"),
        P("loop", "width"),
        P(("groups", "loop"), "width"),
    )
    out_specs = (
        P(("groups", "loop"), "width"),
        P(("groups", "loop"), "width"),
        P(("groups", "width"), "loop"),
        P(("groups", "width"), "loop"),
        P(("groups", "loop"), "width"),
    )
    return jax.shard_map(layer, mesh=mesh, in_specs=in_specs, out_specs=out_specs, check_vma=False)
```

```python
import functools

import jax
import jax.numpy as jnp
from jax import lax
from jax.experimental import pallas as pl
from jax.experimental.pallas import tpu as pltpu
from jax.sharding import PartitionSpec as P

BF16 = jnp.bfloat16
F32 = jnp.float32
LANES = 128
MIB = 1024 * 1024
KERNEL_VMEM = 46 * MIB


def contract_rows(left, right):
    return lax.dot_general(left, right, (((0,), (0,)), ((), ())), preferred_element_type=F32)


def contract_cols(left, right):
    return lax.dot_general(left, right, (((1,), (1,)), ((), ())), preferred_element_type=F32)


def matmul(left, right):
    return jnp.dot(left, right, preferred_element_type=F32)


def block_of(size, most):
    return max(b for b in range(LANES, most + 1, LANES) if size % b == 0)


def ring_order(n):
    return [0] + list(range(1, n, 2)) + [k for k in range(n - 1, 1, -1) if k % 2 == 0]


def ring_perm(n):
    order = ring_order(n)
    return [(order[k], order[(k + 1) % n]) for k in range(n)]


def ring_place(index, n):
    order = ring_order(n)
    place = jnp.int32(0)
    for k in range(n):
        place = jnp.where(index == order[k], k, place)
    return place.astype(jnp.int32)


def ring_gather(own, axis, perm, n):
    slots = [own]
    for _ in range(n - 1):
        slots.append(lax.ppermute(slots[-1], axis, perm))
    return slots


def ring_scatter(slots, axis, perm, n):
    total = slots[1 % n]
    for h in range(1, n):
        got = lax.ppermute(total.astype(BF16), axis, perm)
        total = got.astype(F32) + slots[(h + 1) % n]
    return total


def together(*arrays):
    return lax.optimization_barrier(list(arrays))


def params():
    return pltpu.CompilerParams(vmem_limit_bytes=KERNEL_VMEM)


def cost(flops, moved):
    return pl.CostEstimate(flops=flops // 64, bytes_accessed=moved // 64, transcendentals=0)


def whole():
    return pl.BlockSpec(memory_space=pltpu.VMEM)


def in_hbm():
    return pl.BlockSpec(memory_space=pltpu.HBM)


def number():
    return pl.BlockSpec(memory_space=pltpu.SMEM)


def copies(blocks, held, sems):
    return [pltpu.make_async_copy(block, held.at[k], sems.at[k]) for k, block in enumerate(blocks)]


def start(*lists):
    for group in zip(*lists):
        for copy in group:
            copy.start()


def columns_of(place, shard):
    return pl.ds(pl.multiple_of(place * shard, LANES), shard)


def load_body(parts, place, gate_w, up_w, gate_held, up_held, sems):
    depth, shard = gate_held.shape
    step, columns = depth // parts, columns_of(place[0], shard)
    loads = []
    for n, (source, held) in enumerate(((gate_w, gate_held), (up_w, up_held))):
        for k in range(parts):
            here = pl.ds(k * step, step)
            loads.append(pltpu.make_async_copy(source.at[here, columns], held.at[here], sems.at[n, k]))
            loads[-1].start()
    for copy in loads:
        copy.wait()


def load(place, gate_w, up_w, shard):
    parts, depth = 4, gate_w.shape[0]
    return pl.pallas_call(
        functools.partial(load_body, parts),
        in_specs=[number(), in_hbm(), in_hbm()],
        out_specs=[whole()] * 2,
        out_shape=[jax.ShapeDtypeStruct((depth, shard), gate_w.dtype)] * 2,
        scratch_shapes=[pltpu.SemaphoreType.DMA((2, parts))],
        cost_estimate=cost(0, 4 * depth * shard),
        compiler_params=params(),
        name="load",
    )(place, gate_w, up_w)


def pre_body(parts, place, rows, gate_w, up_w, gate, up, gate_held, up_held, gate_sum, up_sum, sems):
    depth, shard = gate_held.shape[1:]
    columns = columns_of(place[0], shard)
    here = [pl.ds(k * depth, depth) for k in range(parts)]
    gate_in = copies([gate_w.at[h, columns] for h in here], gate_held, sems.at[0])
    up_in = copies([up_w.at[h, columns] for h in here], up_held, sems.at[1])
    start(gate_in, up_in)
    for k in range(parts):
        part = rows[:, k * depth : (k + 1) * depth]
        gate_in[k].wait()
        up_in[k].wait()
        values = matmul(part, gate_held[k]), matmul(part, up_held[k])
        for value, total, out in zip(values, (gate_sum, up_sum), (gate, up)):
            if k:
                value += total[...]
            if k < parts - 1:
                total[...] = value
            else:
                out[...] = value.astype(out.dtype)


def partial_pre(place, rows, gate_w, up_w, shard, dtype):
    tokens, depth = rows.shape
    parts = depth // block_of(depth, 512)
    held = pltpu.VMEM((parts, depth // parts, shard), BF16)
    return pl.pallas_call(
        functools.partial(pre_body, parts),
        in_specs=[number(), whole(), in_hbm(), in_hbm()],
        out_specs=[whole()] * 2,
        out_shape=[jax.ShapeDtypeStruct((tokens, shard), dtype)] * 2,
        scratch_shapes=[held, held]
        + [pltpu.VMEM((tokens, shard), F32)] * 2
        + [pltpu.SemaphoreType.DMA((2, parts))],
        cost_estimate=cost(4 * tokens * depth * shard, 4 * depth * shard),
        compiler_params=params(),
        name="partial_pre",
    )(place, rows, gate_w, up_w)


def grad_body(count, places, rows, down_w, *rest):
    totals, (held, rows_t, sems) = rest[:count], rest[count:]
    shard = held.shape[1]
    loads = copies(
        [down_w.at[pl.ds(pl.multiple_of(places[j] * shard, LANES), shard)] for j in range(count)], held, sems
    )
    start(loads)
    rows_t[...] = rows[...].T
    half = shard // 2
    for j in range(count):
        loads[j].wait()
        low, high = matmul(held[j, :half], rows_t[...]), matmul(held[j, half:], rows_t[...])
        totals[j][...] = jnp.concatenate([low, high], axis=0).T


def partial_hidden_grad(places, rows, down_w, shard):
    count, (tokens, depth) = places.shape[0], rows.shape
    return list(
        pl.pallas_call(
            functools.partial(grad_body, count),
            in_specs=[number(), whole(), in_hbm()],
            out_specs=[whole()] * count,
            out_shape=[jax.ShapeDtypeStruct((tokens, shard), F32)] * count,
            scratch_shapes=[
                pltpu.VMEM((count, shard, depth), BF16),
                pltpu.VMEM((depth, tokens), BF16),
                pltpu.SemaphoreType.DMA((count,)),
            ],
            cost_estimate=cost(2 * count * tokens * depth * shard, 2 * count * depth * shard),
            compiler_params=params(),
            name="partial_hidden_grad",
        )(places, rows, down_w)
    )


def down_body(parts, first, place, hidden, down_w, rows, *rest):
    total, grad, held, made, hidden_t, in_sems, out_sems = rest[-7:]
    shard, step = held.shape[1:]
    units = columns_of(place[0], shard)
    here = [pl.ds(k * step, step) for k in range(parts)]
    loads = copies([down_w.at[units, h] for h in here], held, in_sems)
    start(loads)
    hidden_t[...] = hidden[...].T
    stores = []
    for k in range(parts):
        span = slice(k * step, (k + 1) * step)
        loads[k].wait()
        value, product = matmul(hidden[...], held[k]), matmul(hidden_t[...], rows[:, span])
        made[k] = product.astype(BF16)
        stores.append(pltpu.make_async_copy(made.at[k], grad.at[units, here[k]], out_sems.at[k]))
        stores[k].start()
        total[:, span] = value if first else rest[0][:, span] + value
    for store in stores:
        store.wait()


def down_shard(place, hidden, down_w, rows, before):
    tokens, shard = hidden.shape
    units, depth = down_w.shape
    step = block_of(depth, 512)
    parts = depth // step
    first = before is None
    held = pltpu.VMEM((parts, shard, step), BF16)
    return list(
        pl.pallas_call(
            functools.partial(down_body, parts, first),
            in_specs=[number(), whole(), in_hbm(), whole()] + ([] if first else [whole(), in_hbm()]),
            out_specs=[whole(), in_hbm()],
            out_shape=[
                jax.ShapeDtypeStruct((tokens, depth), F32),
                jax.ShapeDtypeStruct((units, depth), BF16),
            ],
            scratch_shapes=[held, held, pltpu.VMEM((shard, tokens), BF16)] + [pltpu.SemaphoreType.DMA((parts,))] * 2,
            input_output_aliases={} if first else {4: 0, 5: 1},
            cost_estimate=cost(4 * tokens * depth * shard, 4 * depth * shard),
            compiler_params=params(),
            name="down_shard",
        )(place, hidden, down_w, rows, *([] if first else before))
    )


def turn_body(source, out):
    out[...] = source[...].T


def turn(source):
    rows, cols = source.shape
    return pl.pallas_call(
        turn_body,
        in_specs=[whole()],
        out_specs=whole(),
        out_shape=jax.ShapeDtypeStruct((cols, rows), source.dtype),
        cost_estimate=cost(0, 4 * source.size),
        compiler_params=params(),
        name="turn",
    )(source)


def weight_body(parts, place, pre, rows_t, *rest):
    grad, made, sems = rest[-3:]
    step, shard = made.shape[1:]
    half, columns = step // 2, columns_of(place[0], shard)
    stores = []
    for k in range(parts):
        low, high = (matmul(rows_t[pl.ds(k * step + n * half, half)], pre[...]) for n in range(2))
        made[k, :half] = low.astype(BF16)
        made[k, half:] = high.astype(BF16)
        stores.append(pltpu.make_async_copy(made.at[k], grad.at[pl.ds(k * step, step), columns], sems.at[k]))
        stores[k].start()
    for store in stores:
        store.wait()


def weight_shard(place, pre, rows_t, units, before):
    tokens, shard = pre.shape
    depth = rows_t.shape[0]
    step = block_of(depth, 512)
    parts = depth // step
    first = before is None
    return pl.pallas_call(
        functools.partial(weight_body, parts),
        in_specs=[number(), whole(), whole()] + ([] if first else [in_hbm()]),
        out_specs=in_hbm(),
        out_shape=jax.ShapeDtypeStruct((depth, units), BF16),
        scratch_shapes=[pltpu.VMEM((parts, step, shard), BF16), pltpu.SemaphoreType.DMA((parts,))],
        input_output_aliases={} if first else {3: 0},
        cost_estimate=cost(2 * tokens * depth * shard, 2 * depth * shard),
        compiler_params=params(),
        name="weight_shard",
    )(place, pre, rows_t, *([] if first else [before]))


def shards(loop, width, inputs, gate_weight, up_weight, down_weight, out_grad):
    hidden_dev = gate_weight.shape[1]
    shard = hidden_dev // width
    chips = loop // 2
    own_rows = inputs.shape[0]

    z_perm = ring_perm(width)
    y_perm = [(2 * a + core, 2 * b + core) for a, b in ring_perm(chips) for core in (0, 1)]
    core_perm = [(k, k ^ 1) for k in range(loop)]

    def gather_core(mine):
        return jnp.concatenate(mine + [lax.ppermute(m, "loop", core_perm) for m in mine], axis=0)

    def scatter_chips(mine):
        slots = [mine[k * own_rows : (k + 1) * own_rows] for k in range(chips)]
        return ring_scatter(slots, "loop", y_perm, chips).astype(BF16)

    def scatter_loop(total):
        half = chips * own_rows
        return scatter_chips(total[:half] + lax.ppermute(total[half:], "loop", core_perm))

    place = ring_place(lax.axis_index("width"), width)
    places = lax.rem(place + width - jnp.arange(width, dtype=jnp.int32), jnp.int32(width))

    def hop(sent):
        return lax.ppermute(sent, "width", z_perm)

    def add(got, term):
        return got.astype(F32) + term

    def slot_of(array, slot):
        return lax.dynamic_slice_in_dim(array, places[slot] * shard, shard, axis=1)

    def pre_of(slot, rows):
        return partial_pre(places[slot : slot + 1], rows, gate_weight, up_weight, shard, F32)

    gate_held, up_held = load(places[1:2], gate_weight, up_weight, shard)
    mine = ring_gather(inputs, "loop", y_perm, chips)
    out_grad, mine[-1] = together(out_grad, mine[-1])
    gathered = gather_core(mine)
    gate_first, up_first = matmul(gathered, gate_held).astype(BF16), matmul(gathered, up_held).astype(BF16)
    gate, up = hop(gate_first), hop(up_first)
    rows, gate_first, up_first = together(gathered, gate_first, up_first)
    slots = [(k + 1) % width for k in range(width)]
    terms = [None] * width
    terms[slots[1]] = pre_of(slots[1], rows)
    piece = gather_core(ring_gather(out_grad, "loop", y_perm, chips))
    piece, *terms[slots[1]] = together(piece, *terms[slots[1]])
    grad_n = partial_hidden_grad(places, piece, down_weight, shard)
    rows, grad_n[1] = together(rows, grad_n[1])
    for slot in slots[2:]:
        terms[slot] = pre_of(slot, rows)

    for h in range(1, width - 1):
        sums = add(gate, terms[slots[h]][0]).astype(BF16), add(up, terms[slots[h]][1]).astype(BF16)
        if h == width - 2:
            sent, *sums = together(grad_n[1].astype(BF16), *sums)
        gate, up = hop(sums[0]), hop(sums[1])
    if width == 2:
        sent = grad_n[1].astype(BF16)
    hidden_grad = hop(sent)
    gate, up = add(gate, terms[0][0]), add(up, terms[0][1])
    sig = jax.nn.sigmoid(gate)
    hidden = [(gate * sig * up).astype(BF16)]

    down = None
    for h in range(1, width):
        if h < width - 1:
            sent = add(hidden_grad, grad_n[h + 1]).astype(BF16)
            if h == 1:
                sent, hidden[0] = together(sent, hidden[0])
            hidden.append(hop(hidden[-1]))
            hidden_grad = hop(sent)
        else:
            hidden_grad = add(hidden_grad, grad_n[0])
            if width == 2:
                hidden.append(hop(hidden[-1]))
        if h < width - 1:
            down = down_shard(places[h - 1 : h], hidden[h - 1], down_weight, piece, down)

    rows_t = turn(gathered)
    pre_gate = [(hidden_grad * up * sig * (1.0 + gate * (1.0 - sig))).astype(BF16)]
    pre_up = [(hidden_grad * gate * sig).astype(BF16)]
    total, gate_grad, up_grad = 0.0, None, None
    for k in range(width):
        here, last = places[k : k + 1], k == width - 1
        if not last:
            pre_gate.append(hop(pre_gate[k]))
            pre_up.append(hop(pre_up[k]))
        if last:
            output = scatter_loop(down[0])
            arrays = pre_gate[k], pre_up[k], gate_grad, up_grad, output
            pre_gate[k], pre_up[k], gate_grad, up_grad, output = together(*arrays)
        total = total + (
            contract_cols(pre_gate[k], slot_of(gate_weight, k)) + contract_cols(pre_up[k], slot_of(up_weight, k))
        )
        if last:
            break
        gate_grad = weight_shard(here, pre_gate[k], rows_t, hidden_dev, gate_grad)
        up_grad = weight_shard(here, pre_up[k], rows_t, hidden_dev, up_grad)
        if k < width - 2:
            pre_gate[k + 1], total = together(pre_gate[k + 1], total)
            pre_up[k + 1], gate_grad, up_grad = together(pre_up[k + 1], gate_grad, up_grad)
        done = width - 2 + k
        if done < width:
            if len(hidden) < width:
                hidden.append(hop(hidden[-1]))
            down = down_shard(places[done : done + 1], hidden[done], down_weight, piece, down)
    other = lax.ppermute(total[chips * own_rows :], "loop", core_perm)
    pre_last, total = together(pre_gate[-1], total)
    gate_grad = weight_shard(here, pre_last, rows_t, hidden_dev, gate_grad)
    other, gate_grad = together(other, gate_grad)
    input_grad = scatter_chips(total[: chips * own_rows] + other)
    up_grad = weight_shard(here, pre_up[-1], rows_t, hidden_dev, up_grad)
    down_grad = down[1]
    return (output, input_grad, gate_grad, up_grad, down_grad)


def plain(inputs, gate_weight, up_weight, down_weight, out_grad):
    gathered = lax.all_gather(inputs, "loop", axis=0, tiled=True)
    gate = lax.psum(matmul(gathered, gate_weight), "width")
    up = lax.psum(matmul(gathered, up_weight), "width")
    sig = jax.nn.sigmoid(gate)
    hidden = (gate * sig * up).astype(BF16)
    output = lax.psum_scatter(matmul(hidden, down_weight), "loop", scatter_dimension=0, tiled=True).astype(BF16)
    piece = lax.all_gather(out_grad, "loop", axis=0, tiled=True)
    down_grad = contract_rows(hidden, piece).astype(BF16)
    hidden_grad = lax.psum(contract_cols(piece, down_weight), "width")
    pre_gate = (hidden_grad * up * sig * (1.0 + gate * (1.0 - sig))).astype(BF16)
    pre_up = (hidden_grad * gate * sig).astype(BF16)
    input_grad = lax.psum_scatter(
        contract_cols(pre_gate, gate_weight) + contract_cols(pre_up, up_weight),
        "loop",
        scatter_dimension=0,
        tiled=True,
    ).astype(BF16)
    gate_grad = contract_rows(gathered, pre_gate).astype(BF16)
    up_grad = contract_rows(gathered, pre_up).astype(BF16)
    return (output, input_grad, gate_grad, up_grad, down_grad)


def solution(mesh):
    loop, width = mesh.shape["loop"], mesh.shape["width"]

    def layer(*arrays):
        units = arrays[1].shape[1]
        if units % (width * LANES) or loop % 2 or width < 2:
            return plain(*arrays)
        return shards(loop, width, *arrays)

    in_specs = (
        P(("groups", "loop"), "width"),
        P("width", "loop"),
        P("width", "loop"),
        P("loop", "width"),
        P(("groups", "loop"), "width"),
    )
    out_specs = (
        P(("groups", "loop"), "width"),
        P(("groups", "loop"), "width"),
        P(("groups", "width"), "loop"),
        P(("groups", "width"), "loop"),
        P(("groups", "loop"), "width"),
    )
    return jax.shard_map(layer, mesh=mesh, in_specs=in_specs, out_specs=out_specs, check_vma=False)
```

```python
import functools

import jax
import jax.numpy as jnp
from jax import lax
from jax.experimental import pallas as pl
from jax.experimental.pallas import tpu as pltpu
from jax.sharding import PartitionSpec as P

BF16 = jnp.bfloat16
F32 = jnp.float32
LANES = 128
MIB = 1024 * 1024
KERNEL_VMEM = 46 * MIB


def contract_rows(left, right):
    return lax.dot_general(left, right, (((0,), (0,)), ((), ())), preferred_element_type=F32)


def contract_cols(left, right):
    return lax.dot_general(left, right, (((1,), (1,)), ((), ())), preferred_element_type=F32)


def matmul(left, right):
    return jnp.dot(left, right, preferred_element_type=F32)


def block_of(size, most):
    return max(b for b in range(LANES, most + 1, LANES) if size % b == 0)


def ring_order(n):
    return [0] + list(range(1, n, 2)) + [k for k in range(n - 1, 1, -1) if k % 2 == 0]


def ring_perm(n):
    order = ring_order(n)
    return [(order[k], order[(k + 1) % n]) for k in range(n)]


def ring_place(index, n):
    order = ring_order(n)
    place = jnp.int32(0)
    for k in range(n):
        place = jnp.where(index == order[k], k, place)
    return place.astype(jnp.int32)


def ring_gather(own, axis, perm, n):
    slots = [own]
    for _ in range(n - 1):
        slots.append(lax.ppermute(slots[-1], axis, perm))
    return slots


def ring_scatter(slots, axis, perm, n):
    total = slots[1 % n]
    for h in range(1, n):
        got = lax.ppermute(total.astype(BF16), axis, perm)
        total = got.astype(F32) + slots[(h + 1) % n]
    return total


def together(*arrays):
    return lax.optimization_barrier(list(arrays))


def params():
    return pltpu.CompilerParams(vmem_limit_bytes=KERNEL_VMEM)


def cost(flops, moved):
    return pl.CostEstimate(flops=flops // 64, bytes_accessed=moved // 64, transcendentals=0)


def whole():
    return pl.BlockSpec(memory_space=pltpu.VMEM)


def in_hbm():
    return pl.BlockSpec(memory_space=pltpu.HBM)


def number():
    return pl.BlockSpec(memory_space=pltpu.SMEM)


def copies(blocks, held, sems):
    return [pltpu.make_async_copy(block, held.at[k], sems.at[k]) for k, block in enumerate(blocks)]


def start(*lists):
    for group in zip(*lists):
        for copy in group:
            copy.start()


def columns_of(place, shard):
    return pl.ds(pl.multiple_of(place * shard, LANES), shard)


def load_body(parts, place, gate_w, up_w, gate_held, up_held, sems):
    depth, shard = gate_held.shape
    step, columns = depth // parts, columns_of(place[0], shard)
    loads = []
    for n, (source, held) in enumerate(((gate_w, gate_held), (up_w, up_held))):
        for k in range(parts):
            here = pl.ds(k * step, step)
            loads.append(pltpu.make_async_copy(source.at[here, columns], held.at[here], sems.at[n, k]))
            loads[-1].start()
    for copy in loads:
        copy.wait()


def load(place, gate_w, up_w, shard):
    parts, depth = 4, gate_w.shape[0]
    return pl.pallas_call(
        functools.partial(load_body, parts),
        in_specs=[number(), in_hbm(), in_hbm()],
        out_specs=[whole()] * 2,
        out_shape=[jax.ShapeDtypeStruct((depth, shard), gate_w.dtype)] * 2,
        scratch_shapes=[pltpu.SemaphoreType.DMA((2, parts))],
        cost_estimate=cost(0, 4 * depth * shard),
        compiler_params=params(),
        name="load",
    )(place, gate_w, up_w)


def pre_body(parts, place, rows, gate_w, up_w, gate, up, gate_held, up_held, gate_sum, up_sum, sems):
    depth, shard = gate_held.shape[1:]
    columns = columns_of(place[0], shard)
    here = [pl.ds(k * depth, depth) for k in range(parts)]
    gate_in = copies([gate_w.at[h, columns] for h in here], gate_held, sems.at[0])
    up_in = copies([up_w.at[h, columns] for h in here], up_held, sems.at[1])
    start(gate_in, up_in)
    for k in range(parts):
        part = rows[:, k * depth : (k + 1) * depth]
        gate_in[k].wait()
        up_in[k].wait()
        values = matmul(part, gate_held[k]), matmul(part, up_held[k])
        for value, total, out in zip(values, (gate_sum, up_sum), (gate, up)):
            if k:
                value += total[...]
            if k < parts - 1:
                total[...] = value
            else:
                out[...] = value.astype(out.dtype)


def partial_pre(place, rows, gate_w, up_w, shard, dtype):
    tokens, depth = rows.shape
    parts = depth // block_of(depth, 512)
    held = pltpu.VMEM((parts, depth // parts, shard), BF16)
    return pl.pallas_call(
        functools.partial(pre_body, parts),
        in_specs=[number(), whole(), in_hbm(), in_hbm()],
        out_specs=[whole()] * 2,
        out_shape=[jax.ShapeDtypeStruct((tokens, shard), dtype)] * 2,
        scratch_shapes=[held, held]
        + [pltpu.VMEM((tokens, shard), F32)] * 2
        + [pltpu.SemaphoreType.DMA((2, parts))],
        cost_estimate=cost(4 * tokens * depth * shard, 4 * depth * shard),
        compiler_params=params(),
        name="partial_pre",
    )(place, rows, gate_w, up_w)


def grad_body(count, places, rows, down_w, *rest):
    totals, (held, rows_t, sems) = rest[:count], rest[count:]
    shard = held.shape[1]
    loads = copies(
        [down_w.at[pl.ds(pl.multiple_of(places[j] * shard, LANES), shard)] for j in range(count)], held, sems
    )
    start(loads)
    rows_t[...] = rows[...].T
    half = shard // 2
    for j in range(count):
        loads[j].wait()
        low, high = matmul(held[j, :half], rows_t[...]), matmul(held[j, half:], rows_t[...])
        totals[j][...] = jnp.concatenate([low, high], axis=0).T


def partial_hidden_grad(places, rows, down_w, shard):
    count, (tokens, depth) = places.shape[0], rows.shape
    return list(
        pl.pallas_call(
            functools.partial(grad_body, count),
            in_specs=[number(), whole(), in_hbm()],
            out_specs=[whole()] * count,
            out_shape=[jax.ShapeDtypeStruct((tokens, shard), F32)] * count,
            scratch_shapes=[
                pltpu.VMEM((count, shard, depth), BF16),
                pltpu.VMEM((depth, tokens), BF16),
                pltpu.SemaphoreType.DMA((count,)),
            ],
            cost_estimate=cost(2 * count * tokens * depth * shard, 2 * count * depth * shard),
            compiler_params=params(),
            name="partial_hidden_grad",
        )(places, rows, down_w)
    )


def down_body(count, parts, first, places, *rest):
    hidden, (down_w, rows), rest = rest[:count], rest[count : count + 2], rest[count + 2 :]
    total, grad, held, made, flat, turned, in_sems, out_sems = rest[-8:]
    step = held.shape[2]
    shard = held.shape[1] // count
    here = [pl.ds(k * step, step) for k in range(parts)]
    units = [columns_of(places[j], shard) for j in range(count)]
    spans = [pl.ds(j * shard, shard) for j in range(count)]
    loads = [
        [pltpu.make_async_copy(down_w.at[units[j], h], held.at[k, spans[j]], in_sems.at[j, k]) for j in range(count)]
        for k, h in enumerate(here)
    ]
    start(*zip(*loads))
    for j in range(count):
        flat[:, j * shard : (j + 1) * shard] = hidden[j][...]
        turned[j * shard : (j + 1) * shard] = hidden[j][...].T
    stores = []
    for k in range(parts):
        columns = slice(k * step, (k + 1) * step)
        made[k] = matmul(turned[...], rows[:, columns]).astype(BF16)
        for j in range(count):
            stores.append(pltpu.make_async_copy(made.at[k, spans[j]], grad.at[units[j], here[k]], out_sems.at[j, k]))
            stores[-1].start()
            loads[k][j].wait()
        value = matmul(flat[...], held[k])
        total[:, columns] = value if first else rest[0][:, columns] + value
    for store in stores:
        store.wait()


def down_shards(places, hidden, down_w, rows, before):
    count = len(hidden)
    tokens, shard = hidden[0].shape
    units, depth = down_w.shape
    step = block_of(depth, 512)
    parts = depth // step
    first = before is None
    held = pltpu.VMEM((parts, count * shard, step), BF16)
    return list(
        pl.pallas_call(
            functools.partial(down_body, count, parts, first),
            in_specs=[number()] + [whole()] * count + [in_hbm(), whole()] + ([] if first else [whole(), in_hbm()]),
            out_specs=[whole(), in_hbm()],
            out_shape=[
                jax.ShapeDtypeStruct((tokens, depth), F32),
                jax.ShapeDtypeStruct((units, depth), BF16),
            ],
            scratch_shapes=[
                held,
                held,
                pltpu.VMEM((tokens, count * shard), BF16),
                pltpu.VMEM((count * shard, tokens), BF16),
            ]
            + [pltpu.SemaphoreType.DMA((count, parts))] * 2,
            input_output_aliases={} if first else {count + 3: 0, count + 4: 1},
            cost_estimate=cost(4 * count * tokens * depth * shard, 4 * count * depth * shard),
            compiler_params=params(),
            name="down_shards",
        )(places, *hidden, down_w, rows, *([] if first else before))
    )


def both_body(parts, first, writes, place, pre_gate, pre_up, gate_w, up_w, *rest):
    rest = list(rest)
    rows_t = rest.pop(0) if writes else None
    before = None if first else rest.pop(0)
    if writes and not first:
        del rest[:2]
    total = rest.pop(0)
    grads = [rest.pop(0) for _ in range(2)] if writes else []
    held, turned, in_sems = rest[:3]
    step, shard = held.shape[1], held.shape[2] // 2
    half, columns = step // 2, columns_of(place[0], shard)
    here = [pl.ds(k * step, step) for k in range(parts)]
    sides = pl.ds(0, shard), pl.ds(shard, shard)
    loads = [
        [
            pltpu.make_async_copy(source.at[h, columns], held.at[k, :, sides[n]], in_sems.at[n, k])
            for n, source in enumerate((gate_w, up_w))
        ]
        for k, h in enumerate(here)
    ]
    start(*zip(*loads))
    turned[:shard] = pre_gate[...].T
    turned[shard:] = pre_up[...].T
    if writes:
        made, flat, out_sems = rest[3:]
        flat[:, :shard] = pre_gate[...]
        flat[:, shard:] = pre_up[...]
    stores = []
    for k in range(parts):
        span = slice(k * step, (k + 1) * step)
        if writes:
            low, high = (matmul(rows_t[pl.ds(k * step + n * half, half)], flat[...]) for n in range(2))
            made[k, :half] = low.astype(BF16)
            made[k, half:] = high.astype(BF16)
            for n in range(2):
                stores.append(
                    pltpu.make_async_copy(made.at[k, :, sides[n]], grads[n].at[here[k], columns], out_sems.at[n, k])
                )
                stores[-1].start()
        for n in range(2):
            loads[k][n].wait()
        low, high = matmul(held[k, :half], turned[...]), matmul(held[k, half:], turned[...])
        value = jnp.concatenate([low, high], axis=0).T
        total[:, span] = value if first else before[:, span] + value
    for store in stores:
        store.wait()


def input_and_weights(place, pre_gate, pre_up, gate_w, up_w, rows_t, total, grads, writes=True):
    tokens, shard = pre_gate.shape
    depth, units = gate_w.shape
    step = block_of(depth, 512)
    parts = depth // step
    first = total is None
    operands, in_specs = [place, pre_gate, pre_up, gate_w, up_w], [number(), whole(), whole(), in_hbm(), in_hbm()]
    out_specs, out_shape, aliases = [whole()], [jax.ShapeDtypeStruct((tokens, depth), F32)], {}
    held = pltpu.VMEM((parts, step, 2 * shard), BF16)
    scratch = [held, pltpu.VMEM((2 * shard, tokens), BF16), pltpu.SemaphoreType.DMA((2, parts))]
    if writes:
        operands += [rows_t]
        in_specs += [whole()]
        out_specs += [in_hbm()] * 2
        out_shape += [jax.ShapeDtypeStruct((depth, units), BF16)] * 2
        scratch += [held, pltpu.VMEM((tokens, 2 * shard), BF16), pltpu.SemaphoreType.DMA((2, parts))]
    if not first:
        aliases[len(operands)] = 0
        operands += [total]
        in_specs += [whole()]
        if writes:
            aliases.update({len(operands): 1, len(operands) + 1: 2})
            operands += grads
            in_specs += [in_hbm()] * 2
    got = pl.pallas_call(
        functools.partial(both_body, parts, first, writes),
        in_specs=in_specs,
        out_specs=out_specs,
        out_shape=out_shape,
        scratch_shapes=scratch,
        input_output_aliases=aliases,
        cost_estimate=cost(8 * tokens * depth * shard, 8 * depth * shard),
        compiler_params=params(),
        name="input_and_weights" if writes else "input_shard",
    )(*operands)
    return got[0], list(got[1:]) if writes else grads


def turn_body(source, out):
    out[...] = source[...].T


def turn(source):
    rows, cols = source.shape
    return pl.pallas_call(
        turn_body,
        in_specs=[whole()],
        out_specs=whole(),
        out_shape=jax.ShapeDtypeStruct((cols, rows), source.dtype),
        cost_estimate=cost(0, 4 * source.size),
        compiler_params=params(),
        name="turn",
    )(source)


def weight_body(parts, place, pre, rows_t, *rest):
    grad, made, sems = rest[-3:]
    step, shard = made.shape[1:]
    half, columns = step // 2, columns_of(place[0], shard)
    stores = []
    for k in range(parts):
        low, high = (matmul(rows_t[pl.ds(k * step + n * half, half)], pre[...]) for n in range(2))
        made[k, :half] = low.astype(BF16)
        made[k, half:] = high.astype(BF16)
        stores.append(pltpu.make_async_copy(made.at[k], grad.at[pl.ds(k * step, step), columns], sems.at[k]))
        stores[k].start()
    for store in stores:
        store.wait()


def weight_shard(place, pre, rows_t, units, before):
    tokens, shard = pre.shape
    depth = rows_t.shape[0]
    step = block_of(depth, 512)
    parts = depth // step
    first = before is None
    return pl.pallas_call(
        functools.partial(weight_body, parts),
        in_specs=[number(), whole(), whole()] + ([] if first else [in_hbm()]),
        out_specs=in_hbm(),
        out_shape=jax.ShapeDtypeStruct((depth, units), BF16),
        scratch_shapes=[pltpu.VMEM((parts, step, shard), BF16), pltpu.SemaphoreType.DMA((parts,))],
        input_output_aliases={} if first else {3: 0},
        cost_estimate=cost(2 * tokens * depth * shard, 2 * depth * shard),
        compiler_params=params(),
        name="weight_shard",
    )(place, pre, rows_t, *([] if first else [before]))


def shards(loop, width, inputs, gate_weight, up_weight, down_weight, out_grad):
    hidden_dev = gate_weight.shape[1]
    shard = hidden_dev // width
    chips = loop // 2
    own_rows = inputs.shape[0]

    z_perm = ring_perm(width)
    y_perm = [(2 * a + core, 2 * b + core) for a, b in ring_perm(chips) for core in (0, 1)]
    core_perm = [(k, k ^ 1) for k in range(loop)]

    def gather_core(mine):
        return jnp.concatenate(mine + [lax.ppermute(m, "loop", core_perm) for m in mine], axis=0)

    def scatter_chips(mine):
        slots = [mine[k * own_rows : (k + 1) * own_rows] for k in range(chips)]
        return ring_scatter(slots, "loop", y_perm, chips).astype(BF16)

    def scatter_loop(total):
        half = chips * own_rows
        return scatter_chips(total[:half] + lax.ppermute(total[half:], "loop", core_perm))

    place = ring_place(lax.axis_index("width"), width)
    places = lax.rem(place + width - jnp.arange(width, dtype=jnp.int32), jnp.int32(width))

    def hop(sent):
        return lax.ppermute(sent, "width", z_perm)

    def add(got, term):
        return got.astype(F32) + term

    def slot_of(array, slot):
        return lax.dynamic_slice_in_dim(array, places[slot] * shard, shard, axis=1)

    def pre_of(slot, rows):
        return partial_pre(places[slot : slot + 1], rows, gate_weight, up_weight, shard, F32)

    gate_held, up_held = load(places[1:2], gate_weight, up_weight, shard)
    mine = ring_gather(inputs, "loop", y_perm, chips)
    out_grad, mine[-1] = together(out_grad, mine[-1])
    gathered = gather_core(mine)
    gate_first, up_first = matmul(gathered, gate_held).astype(BF16), matmul(gathered, up_held).astype(BF16)
    gate, up = hop(gate_first), hop(up_first)
    rows, gate_first, up_first = together(gathered, gate_first, up_first)
    slots = [(k + 1) % width for k in range(width)]
    terms = [None] * width
    terms[slots[1]] = pre_of(slots[1], rows)
    piece = gather_core(ring_gather(out_grad, "loop", y_perm, chips))
    piece, *terms[slots[1]] = together(piece, *terms[slots[1]])
    grad_n = partial_hidden_grad(places, piece, down_weight, shard)
    rows, grad_n[1] = together(rows, grad_n[1])
    for slot in slots[2:]:
        terms[slot] = pre_of(slot, rows)

    sent = grad_n[1].astype(BF16)
    for h in range(1, width - 1):
        got = hop(sent)
        gate = hop(add(gate, terms[slots[h]][0]).astype(BF16))
        up = hop(add(up, terms[slots[h]][1]).astype(BF16))
        sent = add(got, grad_n[h + 1]).astype(BF16)
    gate, up = add(gate, terms[0][0]), add(up, terms[0][1])
    sig = jax.nn.sigmoid(gate)
    sent, hidden_own = together(sent, (gate * sig * up).astype(BF16))
    hidden_grad = add(hop(sent), grad_n[0])
    hidden = [hidden_own, hop(hidden_own)]

    rows_t = turn(gathered)
    pre_gate = [(hidden_grad * up * sig * (1.0 + gate * (1.0 - sig))).astype(BF16)]
    pre_up = [(hidden_grad * gate * sig).astype(BF16)]
    down, total, grads = None, None, None
    early = range(width - 2)
    for k in range(width):
        last = k == width - 1
        if not last:
            pre_gate[k], pre_up[k], hidden[k + 1] = together(pre_gate[k], pre_up[k], hidden[k + 1])
            if k in early:
                hidden.append(hop(hidden[k + 1]))
            pre_gate.append(hop(pre_gate[k]))
            pre_up.append(hop(pre_up[k]))
        else:
            pre_gate[k], pre_up[k], total, down[0] = together(pre_gate[k], pre_up[k], total, down[0])
            output = scatter_loop(down[0])
        args = places[k : k + 1], pre_gate[k], pre_up[k], gate_weight, up_weight, rows_t, total, grads
        total, grads = input_and_weights(*args, writes=not last)
        ready = slice(k, k + 2) if k % 2 == 0 else slice(k + 1, k + 1)
        if k == width - 2 and k % 2:
            ready = slice(k + 1, k + 2)
        if not last and ready.start < ready.stop:
            down = down_shards(places[ready], hidden[ready], down_weight, piece, down)
            if k in early:
                hidden[k + 2], down[0] = together(hidden[k + 2], down[0])
        if k < width - 2:
            pre_gate[k + 1], pre_up[k + 1], total = together(pre_gate[k + 1], pre_up[k + 1], total)
    gate_grad, up_grad = grads
    other = lax.ppermute(total[chips * own_rows :], "loop", core_perm)
    pre_last, total = together(pre_gate[-1], total)
    gate_grad = weight_shard(places[width - 1 :], pre_last, rows_t, hidden_dev, gate_grad)
    other, gate_grad = together(other, gate_grad)
    input_grad = scatter_chips(total[: chips * own_rows] + other)
    pre_last, output = together(pre_up[-1], output)
    up_grad = weight_shard(places[width - 1 :], pre_last, rows_t, hidden_dev, up_grad)
    down_grad = down[1]
    return (output, input_grad, gate_grad, up_grad, down_grad)


def plain(inputs, gate_weight, up_weight, down_weight, out_grad):
    gathered = lax.all_gather(inputs, "loop", axis=0, tiled=True)
    gate = lax.psum(matmul(gathered, gate_weight), "width")
    up = lax.psum(matmul(gathered, up_weight), "width")
    sig = jax.nn.sigmoid(gate)
    hidden = (gate * sig * up).astype(BF16)
    output = lax.psum_scatter(matmul(hidden, down_weight), "loop", scatter_dimension=0, tiled=True).astype(BF16)
    piece = lax.all_gather(out_grad, "loop", axis=0, tiled=True)
    down_grad = contract_rows(hidden, piece).astype(BF16)
    hidden_grad = lax.psum(contract_cols(piece, down_weight), "width")
    pre_gate = (hidden_grad * up * sig * (1.0 + gate * (1.0 - sig))).astype(BF16)
    pre_up = (hidden_grad * gate * sig).astype(BF16)
    input_grad = lax.psum_scatter(
        contract_cols(pre_gate, gate_weight) + contract_cols(pre_up, up_weight),
        "loop",
        scatter_dimension=0,
        tiled=True,
    ).astype(BF16)
    gate_grad = contract_rows(gathered, pre_gate).astype(BF16)
    up_grad = contract_rows(gathered, pre_up).astype(BF16)
    return (output, input_grad, gate_grad, up_grad, down_grad)


def solution(mesh):
    loop, width = mesh.shape["loop"], mesh.shape["width"]

    def layer(*arrays):
        units = arrays[1].shape[1]
        if units % (width * LANES) or loop % 2 or width < 2:
            return plain(*arrays)
        return shards(loop, width, *arrays)

    in_specs = (
        P(("groups", "loop"), "width"),
        P("width", "loop"),
        P("width", "loop"),
        P("loop", "width"),
        P(("groups", "loop"), "width"),
    )
    out_specs = (
        P(("groups", "loop"), "width"),
        P(("groups", "loop"), "width"),
        P(("groups", "width"), "loop"),
        P(("groups", "width"), "loop"),
        P(("groups", "loop"), "width"),
    )
    return jax.shard_map(layer, mesh=mesh, in_specs=in_specs, out_specs=out_specs, check_vma=False)
```

```python
import functools

import jax
import jax.numpy as jnp
from jax import lax
from jax.experimental import pallas as pl
from jax.experimental.pallas import tpu as pltpu
from jax.sharding import PartitionSpec as P

BF16 = jnp.bfloat16
F32 = jnp.float32
LANES = 128
MIB = 1024 * 1024
KERNEL_VMEM = 46 * MIB


def contract_rows(left, right):
    return lax.dot_general(left, right, (((0,), (0,)), ((), ())), preferred_element_type=F32)


def contract_cols(left, right):
    return lax.dot_general(left, right, (((1,), (1,)), ((), ())), preferred_element_type=F32)


def matmul(left, right):
    return jnp.dot(left, right, preferred_element_type=F32)


def block_of(size, most):
    return max(b for b in range(LANES, most + 1, LANES) if size % b == 0)


def ring_order(n):
    return [0] + list(range(1, n, 2)) + [k for k in range(n - 1, 1, -1) if k % 2 == 0]


def ring_perm(n):
    order = ring_order(n)
    return [(order[k], order[(k + 1) % n]) for k in range(n)]


def ring_place(index, n):
    order = ring_order(n)
    place = jnp.int32(0)
    for k in range(n):
        place = jnp.where(index == order[k], k, place)
    return place.astype(jnp.int32)


def ring_gather(own, axis, perm, n):
    slots = [own]
    for _ in range(n - 1):
        slots.append(lax.ppermute(slots[-1], axis, perm))
    return slots


def ring_scatter(slots, axis, perm, n):
    total = slots[1 % n]
    for h in range(1, n):
        got = lax.ppermute(total.astype(BF16), axis, perm)
        total = got.astype(F32) + slots[(h + 1) % n]
    return total


def together(*arrays):
    return lax.optimization_barrier(list(arrays))


def params():
    return pltpu.CompilerParams(vmem_limit_bytes=KERNEL_VMEM)


def cost(flops, moved):
    return pl.CostEstimate(flops=flops // 64, bytes_accessed=moved // 64, transcendentals=0)


def whole():
    return pl.BlockSpec(memory_space=pltpu.VMEM)


def in_hbm():
    return pl.BlockSpec(memory_space=pltpu.HBM)


def number():
    return pl.BlockSpec(memory_space=pltpu.SMEM)


def copies(blocks, held, sems):
    return [pltpu.make_async_copy(block, held.at[k], sems.at[k]) for k, block in enumerate(blocks)]


def start(*lists):
    for group in zip(*lists):
        for copy in group:
            copy.start()


def columns_of(place, shard):
    return pl.ds(pl.multiple_of(place * shard, LANES), shard)


def load_body(parts, place, gate_w, up_w, gate_held, up_held, sems):
    depth, shard = gate_held.shape
    step, columns = depth // parts, columns_of(place[0], shard)
    loads = []
    for n, (source, held) in enumerate(((gate_w, gate_held), (up_w, up_held))):
        for k in range(parts):
            here = pl.ds(k * step, step)
            loads.append(pltpu.make_async_copy(source.at[here, columns], held.at[here], sems.at[n, k]))
            loads[-1].start()
    for copy in loads:
        copy.wait()


def load(place, gate_w, up_w, shard):
    parts, depth = 4, gate_w.shape[0]
    return pl.pallas_call(
        functools.partial(load_body, parts),
        in_specs=[number(), in_hbm(), in_hbm()],
        out_specs=[whole()] * 2,
        out_shape=[jax.ShapeDtypeStruct((depth, shard), gate_w.dtype)] * 2,
        scratch_shapes=[pltpu.SemaphoreType.DMA((2, parts))],
        cost_estimate=cost(0, 4 * depth * shard),
        compiler_params=params(),
        name="load",
    )(place, gate_w, up_w)


def pre_body(parts, place, rows, gate_w, up_w, gate, up, gate_held, up_held, gate_sum, up_sum, sems):
    depth, shard = gate_held.shape[1:]
    columns = columns_of(place[0], shard)
    here = [pl.ds(k * depth, depth) for k in range(parts)]
    gate_in = copies([gate_w.at[h, columns] for h in here], gate_held, sems.at[0])
    up_in = copies([up_w.at[h, columns] for h in here], up_held, sems.at[1])
    start(gate_in, up_in)
    for k in range(parts):
        part = rows[:, k * depth : (k + 1) * depth]
        gate_in[k].wait()
        up_in[k].wait()
        values = matmul(part, gate_held[k]), matmul(part, up_held[k])
        for value, total, out in zip(values, (gate_sum, up_sum), (gate, up)):
            if k:
                value += total[...]
            if k < parts - 1:
                total[...] = value
            else:
                out[...] = value.astype(out.dtype)


def partial_pre(place, rows, gate_w, up_w, shard, dtype):
    tokens, depth = rows.shape
    parts = depth // block_of(depth, 512)
    held = pltpu.VMEM((parts, depth // parts, shard), BF16)
    return pl.pallas_call(
        functools.partial(pre_body, parts),
        in_specs=[number(), whole(), in_hbm(), in_hbm()],
        out_specs=[whole()] * 2,
        out_shape=[jax.ShapeDtypeStruct((tokens, shard), dtype)] * 2,
        scratch_shapes=[held, held]
        + [pltpu.VMEM((tokens, shard), F32)] * 2
        + [pltpu.SemaphoreType.DMA((2, parts))],
        cost_estimate=cost(4 * tokens * depth * shard, 4 * depth * shard),
        compiler_params=params(),
        name="partial_pre",
    )(place, rows, gate_w, up_w)


def grad_body(count, places, rows, down_w, *rest):
    totals, (held, rows_t, sems) = rest[:count], rest[count:]
    shard = held.shape[1]
    loads = copies(
        [down_w.at[pl.ds(pl.multiple_of(places[j] * shard, LANES), shard)] for j in range(count)], held, sems
    )
    start(loads)
    rows_t[...] = rows[...].T
    half = shard // 2
    for j in range(count):
        loads[j].wait()
        low, high = matmul(held[j, :half], rows_t[...]), matmul(held[j, half:], rows_t[...])
        totals[j][...] = jnp.concatenate([low, high], axis=0).T


def partial_hidden_grad(places, rows, down_w, shard):
    count, (tokens, depth) = places.shape[0], rows.shape
    return list(
        pl.pallas_call(
            functools.partial(grad_body, count),
            in_specs=[number(), whole(), in_hbm()],
            out_specs=[whole()] * count,
            out_shape=[jax.ShapeDtypeStruct((tokens, shard), F32)] * count,
            scratch_shapes=[
                pltpu.VMEM((count, shard, depth), BF16),
                pltpu.VMEM((depth, tokens), BF16),
                pltpu.SemaphoreType.DMA((count,)),
            ],
            cost_estimate=cost(2 * count * tokens * depth * shard, 2 * count * depth * shard),
            compiler_params=params(),
            name="partial_hidden_grad",
        )(places, rows, down_w)
    )


def down_body(parts, first, place, hidden, down_w, rows, *rest):
    total, grad, held, made, hidden_t, in_sems, out_sems = rest[-7:]
    shard, step = held.shape[1:]
    units = columns_of(place[0], shard)
    here = [pl.ds(k * step, step) for k in range(parts)]
    loads = copies([down_w.at[units, h] for h in here], held, in_sems)
    start(loads)
    hidden_t[...] = hidden[...].T
    stores = []
    for k in range(parts):
        span = slice(k * step, (k + 1) * step)
        made[k] = matmul(hidden_t[...], rows[:, span]).astype(BF16)
        stores.append(pltpu.make_async_copy(made.at[k], grad.at[units, here[k]], out_sems.at[k]))
        stores[k].start()
        loads[k].wait()
        value = matmul(hidden[...], held[k])
        total[:, span] = value if first else rest[0][:, span] + value
    for store in stores:
        store.wait()


def down_shard(place, hidden, down_w, rows, before):
    tokens, shard = hidden.shape
    units, depth = down_w.shape
    step = block_of(depth, 512)
    parts = depth // step
    first = before is None
    held = pltpu.VMEM((parts, shard, step), BF16)
    return list(
        pl.pallas_call(
            functools.partial(down_body, parts, first),
            in_specs=[number(), whole(), in_hbm(), whole()] + ([] if first else [whole(), in_hbm()]),
            out_specs=[whole(), in_hbm()],
            out_shape=[
                jax.ShapeDtypeStruct((tokens, depth), F32),
                jax.ShapeDtypeStruct((units, depth), BF16),
            ],
            scratch_shapes=[held, held, pltpu.VMEM((shard, tokens), BF16)] + [pltpu.SemaphoreType.DMA((parts,))] * 2,
            input_output_aliases={} if first else {4: 0, 5: 1},
            cost_estimate=cost(4 * tokens * depth * shard, 4 * depth * shard),
            compiler_params=params(),
            name="down_shard",
        )(place, hidden, down_w, rows, *([] if first else before))
    )


def both_body(parts, first, writes, place, pre_gate, pre_up, gate_w, up_w, *rest):
    rest = list(rest)
    rows_t = rest.pop(0) if writes else None
    before = None if first else rest.pop(0)
    if writes and not first:
        del rest[:2]
    total = rest.pop(0)
    grads = [rest.pop(0) for _ in range(2)] if writes else []
    held, turned, in_sems = rest[:3]
    step, shard = held.shape[1], held.shape[2] // 2
    half, columns = step // 2, columns_of(place[0], shard)
    here = [pl.ds(k * step, step) for k in range(parts)]
    sides = pl.ds(0, shard), pl.ds(shard, shard)
    loads = [
        [
            pltpu.make_async_copy(source.at[h, columns], held.at[k, :, sides[n]], in_sems.at[n, k])
            for n, source in enumerate((gate_w, up_w))
        ]
        for k, h in enumerate(here)
    ]
    start(*zip(*loads))
    turned[:shard] = pre_gate[...].T
    turned[shard:] = pre_up[...].T
    if writes:
        made, flat, out_sems = rest[3:]
        flat[:, :shard] = pre_gate[...]
        flat[:, shard:] = pre_up[...]
    stores = []
    for k in range(parts):
        span = slice(k * step, (k + 1) * step)
        if writes:
            low, high = (matmul(rows_t[pl.ds(k * step + n * half, half)], flat[...]) for n in range(2))
            made[k, :half] = low.astype(BF16)
            made[k, half:] = high.astype(BF16)
            for n in range(2):
                stores.append(
                    pltpu.make_async_copy(made.at[k, :, sides[n]], grads[n].at[here[k], columns], out_sems.at[n, k])
                )
                stores[-1].start()
        for n in range(2):
            loads[k][n].wait()
        low, high = matmul(held[k, :half], turned[...]), matmul(held[k, half:], turned[...])
        value = jnp.concatenate([low, high], axis=0).T
        total[:, span] = value if first else before[:, span] + value
    for store in stores:
        store.wait()


def input_and_weights(place, pre_gate, pre_up, gate_w, up_w, rows_t, total, grads, writes=True):
    tokens, shard = pre_gate.shape
    depth, units = gate_w.shape
    step = block_of(depth, 512)
    parts = depth // step
    first = total is None
    operands, in_specs = [place, pre_gate, pre_up, gate_w, up_w], [number(), whole(), whole(), in_hbm(), in_hbm()]
    out_specs, out_shape, aliases = [whole()], [jax.ShapeDtypeStruct((tokens, depth), F32)], {}
    held = pltpu.VMEM((parts, step, 2 * shard), BF16)
    scratch = [held, pltpu.VMEM((2 * shard, tokens), BF16), pltpu.SemaphoreType.DMA((2, parts))]
    if writes:
        operands += [rows_t]
        in_specs += [whole()]
        out_specs += [in_hbm()] * 2
        out_shape += [jax.ShapeDtypeStruct((depth, units), BF16)] * 2
        scratch += [held, pltpu.VMEM((tokens, 2 * shard), BF16), pltpu.SemaphoreType.DMA((2, parts))]
    if not first:
        aliases[len(operands)] = 0
        operands += [total]
        in_specs += [whole()]
        if writes:
            aliases.update({len(operands): 1, len(operands) + 1: 2})
            operands += grads
            in_specs += [in_hbm()] * 2
    got = pl.pallas_call(
        functools.partial(both_body, parts, first, writes),
        in_specs=in_specs,
        out_specs=out_specs,
        out_shape=out_shape,
        scratch_shapes=scratch,
        input_output_aliases=aliases,
        cost_estimate=cost(8 * tokens * depth * shard, 8 * depth * shard),
        compiler_params=params(),
        name="input_and_weights" if writes else "input_shard",
    )(*operands)
    return got[0], list(got[1:]) if writes else grads


def turn_body(source, out):
    out[...] = source[...].T


def turn(source):
    rows, cols = source.shape
    return pl.pallas_call(
        turn_body,
        in_specs=[whole()],
        out_specs=whole(),
        out_shape=jax.ShapeDtypeStruct((cols, rows), source.dtype),
        cost_estimate=cost(0, 4 * source.size),
        compiler_params=params(),
        name="turn",
    )(source)


def weight_body(parts, place, pre, rows_t, *rest):
    grad, made, sems = rest[-3:]
    step, shard = made.shape[1:]
    half, columns = step // 2, columns_of(place[0], shard)
    stores = []
    for k in range(parts):
        low, high = (matmul(rows_t[pl.ds(k * step + n * half, half)], pre[...]) for n in range(2))
        made[k, :half] = low.astype(BF16)
        made[k, half:] = high.astype(BF16)
        stores.append(pltpu.make_async_copy(made.at[k], grad.at[pl.ds(k * step, step), columns], sems.at[k]))
        stores[k].start()
    for store in stores:
        store.wait()


def weight_shard(place, pre, rows_t, units, before):
    tokens, shard = pre.shape
    depth = rows_t.shape[0]
    step = block_of(depth, 512)
    parts = depth // step
    first = before is None
    return pl.pallas_call(
        functools.partial(weight_body, parts),
        in_specs=[number(), whole(), whole()] + ([] if first else [in_hbm()]),
        out_specs=in_hbm(),
        out_shape=jax.ShapeDtypeStruct((depth, units), BF16),
        scratch_shapes=[pltpu.VMEM((parts, step, shard), BF16), pltpu.SemaphoreType.DMA((parts,))],
        input_output_aliases={} if first else {3: 0},
        cost_estimate=cost(2 * tokens * depth * shard, 2 * depth * shard),
        compiler_params=params(),
        name="weight_shard",
    )(place, pre, rows_t, *([] if first else [before]))


def shards(loop, width, inputs, gate_weight, up_weight, down_weight, out_grad):
    hidden_dev = gate_weight.shape[1]
    shard = hidden_dev // width
    chips = loop // 2
    own_rows = inputs.shape[0]

    z_perm = ring_perm(width)
    y_perm = [(2 * a + core, 2 * b + core) for a, b in ring_perm(chips) for core in (0, 1)]
    core_perm = [(k, k ^ 1) for k in range(loop)]

    def gather_core(mine):
        return jnp.concatenate(mine + [lax.ppermute(m, "loop", core_perm) for m in mine], axis=0)

    def scatter_chips(mine):
        slots = [mine[k * own_rows : (k + 1) * own_rows] for k in range(chips)]
        return ring_scatter(slots, "loop", y_perm, chips).astype(BF16)

    def scatter_core(total):
        half = chips * own_rows
        return total[:half] + lax.ppermute(total[half:], "loop", core_perm)

    place = ring_place(lax.axis_index("width"), width)
    places = lax.rem(place + width - jnp.arange(width, dtype=jnp.int32), jnp.int32(width))

    def hop(sent):
        return lax.ppermute(sent, "width", z_perm)

    def add(got, term):
        return got.astype(F32) + term

    def slot_of(array, slot):
        return lax.dynamic_slice_in_dim(array, places[slot] * shard, shard, axis=1)

    def pre_of(slot, rows):
        return partial_pre(places[slot : slot + 1], rows, gate_weight, up_weight, shard, F32)

    gate_held, up_held = load(places[1:2], gate_weight, up_weight, shard)
    mine = ring_gather(inputs, "loop", y_perm, chips)
    out_grad, mine[-1] = together(out_grad, mine[-1])
    gathered = gather_core(mine)
    gate_first, up_first = matmul(gathered, gate_held).astype(BF16), matmul(gathered, up_held).astype(BF16)
    gate, up = hop(gate_first), hop(up_first)
    rows, gate_first, up_first = together(gathered, gate_first, up_first)
    slots = [(k + 1) % width for k in range(width)]
    terms = [None] * width
    terms[slots[1]] = pre_of(slots[1], rows)
    piece = gather_core(ring_gather(out_grad, "loop", y_perm, chips))
    piece, *terms[slots[1]] = together(piece, *terms[slots[1]])
    grad_n = {1: partial_hidden_grad(places[1:2], piece, down_weight, shard)[0]}
    gate, up = add(gate, terms[slots[1]][0]).astype(BF16), add(up, terms[slots[1]][1]).astype(BF16)
    if width > 2:
        rows, piece, gate, up = together(rows, piece, gate, up)
    for slot in slots[2:3]:
        terms[slot] = pre_of(slot, rows)
        piece, *terms[slot] = together(piece, *terms[slot])
    order = jnp.concatenate([places[2:], places[:1]])
    grad_n.update(zip(slots[1:], partial_hidden_grad(order, piece, down_weight, shard)))
    rows, grad_n[slots[1]] = together(rows, grad_n[slots[1]])
    for slot in slots[3:]:
        terms[slot] = pre_of(slot, rows)

    sent = grad_n[1].astype(BF16)
    for h in range(1, width - 1):
        got = hop(sent)
        gate, up = hop(gate), hop(up)
        if h < width - 2:
            gate, up = add(gate, terms[slots[h + 1]][0]).astype(BF16), add(up, terms[slots[h + 1]][1]).astype(BF16)
        sent = add(got, grad_n[h + 1]).astype(BF16)
    gate, up = add(gate, terms[0][0]), add(up, terms[0][1])
    sig = jax.nn.sigmoid(gate)
    sent, hidden_own = together(sent, (gate * sig * up).astype(BF16))
    hidden_grad = add(hop(sent), grad_n[0])
    hidden = [hidden_own, hop(hidden_own)]

    rows_t = turn(gathered)
    down = down_shard(places[:1], hidden[0], down_weight, piece, None)
    pre_gate = [(hidden_grad * up * sig * (1.0 + gate * (1.0 - sig))).astype(BF16)]
    pre_up = [(hidden_grad * gate * sig).astype(BF16)]
    pre_gate[0], down[0] = together(pre_gate[0], down[0])
    total, grads = None, None
    for k in range(width - 1):
        pre_gate.append(hop(pre_gate[k]))
        pre_up.append(hop(pre_up[k]))
        if k < width - 3:
            hidden.append(hop(hidden[k + 1]))
        args = places[k : k + 1], pre_gate[k], pre_up[k], gate_weight, up_weight, rows_t, total, grads
        total, grads = input_and_weights(*args)
        if k < width - 2:
            down = down_shard(places[k + 1 : k + 2], hidden[k + 1], down_weight, piece, down)
            pre_gate[k + 1], total = together(pre_gate[k + 1], total)
            pre_up[k + 1], down[0] = together(pre_up[k + 1], down[0])
    if width > 2:
        hidden[-1], total = together(hidden[-1], total)
        hidden.append(hop(hidden[-1]))
    here = places[width - 1 :]
    total, _ = input_and_weights(
        here, pre_gate[-1], pre_up[-1], gate_weight, up_weight, rows_t, total, grads, writes=False
    )
    hidden[-1], total = together(hidden[-1], total)
    input_mine = scatter_core(total)
    down = down_shard(here, hidden[-1], down_weight, piece, down)
    output_mine = scatter_core(down[0])
    pre_gate[-1], input_mine = together(pre_gate[-1], input_mine)
    pre_up[-1], output_mine = together(pre_up[-1], output_mine)
    input_grad, output = scatter_chips(input_mine), scatter_chips(output_mine)
    gate_grad = weight_shard(here, pre_gate[-1], rows_t, hidden_dev, grads[0])
    up_grad = weight_shard(here, pre_up[-1], rows_t, hidden_dev, grads[1])
    down_grad = down[1]
    return (output, input_grad, gate_grad, up_grad, down_grad)


def plain(inputs, gate_weight, up_weight, down_weight, out_grad):
    gathered = lax.all_gather(inputs, "loop", axis=0, tiled=True)
    gate = lax.psum(matmul(gathered, gate_weight), "width")
    up = lax.psum(matmul(gathered, up_weight), "width")
    sig = jax.nn.sigmoid(gate)
    hidden = (gate * sig * up).astype(BF16)
    output = lax.psum_scatter(matmul(hidden, down_weight), "loop", scatter_dimension=0, tiled=True).astype(BF16)
    piece = lax.all_gather(out_grad, "loop", axis=0, tiled=True)
    down_grad = contract_rows(hidden, piece).astype(BF16)
    hidden_grad = lax.psum(contract_cols(piece, down_weight), "width")
    pre_gate = (hidden_grad * up * sig * (1.0 + gate * (1.0 - sig))).astype(BF16)
    pre_up = (hidden_grad * gate * sig).astype(BF16)
    input_grad = lax.psum_scatter(
        contract_cols(pre_gate, gate_weight) + contract_cols(pre_up, up_weight),
        "loop",
        scatter_dimension=0,
        tiled=True,
    ).astype(BF16)
    gate_grad = contract_rows(gathered, pre_gate).astype(BF16)
    up_grad = contract_rows(gathered, pre_up).astype(BF16)
    return (output, input_grad, gate_grad, up_grad, down_grad)


def solution(mesh):
    loop, width = mesh.shape["loop"], mesh.shape["width"]

    def layer(*arrays):
        units = arrays[1].shape[1]
        if units % (width * LANES) or loop % 2 or width < 2:
            return plain(*arrays)
        return shards(loop, width, *arrays)

    in_specs = (
        P(("groups", "loop"), "width"),
        P("width", "loop"),
        P("width", "loop"),
        P("loop", "width"),
        P(("groups", "loop"), "width"),
    )
    out_specs = (
        P(("groups", "loop"), "width"),
        P(("groups", "loop"), "width"),
        P(("groups", "width"), "loop"),
        P(("groups", "width"), "loop"),
        P(("groups", "loop"), "width"),
    )
    return jax.shard_map(layer, mesh=mesh, in_specs=in_specs, out_specs=out_specs, check_vma=False)
```

```python
import functools

import jax
import jax.numpy as jnp
from jax import lax
from jax.experimental import pallas as pl
from jax.experimental.pallas import tpu as pltpu
from jax.sharding import PartitionSpec as P

BF16 = jnp.bfloat16
F32 = jnp.float32
LANES = 128
MIB = 1024 * 1024
KERNEL_VMEM = 46 * MIB


def contract_rows(left, right):
    return lax.dot_general(left, right, (((0,), (0,)), ((), ())), preferred_element_type=F32)


def contract_cols(left, right):
    return lax.dot_general(left, right, (((1,), (1,)), ((), ())), preferred_element_type=F32)


def matmul(left, right):
    return jnp.dot(left, right, preferred_element_type=F32)


def block_of(size, most):
    return max(b for b in range(LANES, most + 1, LANES) if size % b == 0)


def ring_order(n):
    return [0] + list(range(1, n, 2)) + [k for k in range(n - 1, 1, -1) if k % 2 == 0]


def ring_perm(n):
    order = ring_order(n)
    return [(order[k], order[(k + 1) % n]) for k in range(n)]


def ring_place(index, n):
    order = ring_order(n)
    place = jnp.int32(0)
    for k in range(n):
        place = jnp.where(index == order[k], k, place)
    return place.astype(jnp.int32)


def ring_gather(own, axis, perm, n):
    slots = [own]
    for _ in range(n - 1):
        slots.append(lax.ppermute(slots[-1], axis, perm))
    return slots


def ring_scatter(slots, axis, perm, n):
    total = slots[1 % n]
    for h in range(1, n):
        got = lax.ppermute(total.astype(BF16), axis, perm)
        total = got.astype(F32) + slots[(h + 1) % n]
    return total


def together(*arrays):
    return lax.optimization_barrier(list(arrays))


def params():
    return pltpu.CompilerParams(vmem_limit_bytes=KERNEL_VMEM)


def cost(flops, moved):
    return pl.CostEstimate(flops=flops // 64, bytes_accessed=moved // 64, transcendentals=0)


def whole():
    return pl.BlockSpec(memory_space=pltpu.VMEM)


def in_hbm():
    return pl.BlockSpec(memory_space=pltpu.HBM)


def number():
    return pl.BlockSpec(memory_space=pltpu.SMEM)


def copies(blocks, held, sems):
    return [pltpu.make_async_copy(block, held.at[k], sems.at[k]) for k, block in enumerate(blocks)]


def start(*lists):
    for group in zip(*lists):
        for copy in group:
            copy.start()


def columns_of(place, shard):
    return pl.ds(pl.multiple_of(place * shard, LANES), shard)


def load_body(parts, place, gate_w, up_w, gate_held, up_held, sems):
    depth, shard = gate_held.shape
    step, columns = depth // parts, columns_of(place[0], shard)
    loads = []
    for n, (source, held) in enumerate(((gate_w, gate_held), (up_w, up_held))):
        for k in range(parts):
            here = pl.ds(k * step, step)
            loads.append(pltpu.make_async_copy(source.at[here, columns], held.at[here], sems.at[n, k]))
            loads[-1].start()
    for copy in loads:
        copy.wait()


def load(place, gate_w, up_w, shard):
    parts, depth = 4, gate_w.shape[0]
    return pl.pallas_call(
        functools.partial(load_body, parts),
        in_specs=[number(), in_hbm(), in_hbm()],
        out_specs=[whole()] * 2,
        out_shape=[jax.ShapeDtypeStruct((depth, shard), gate_w.dtype)] * 2,
        scratch_shapes=[pltpu.SemaphoreType.DMA((2, parts))],
        cost_estimate=cost(0, 4 * depth * shard),
        compiler_params=params(),
        name="load",
    )(place, gate_w, up_w)


def pre_body(parts, place, rows, gate_w, up_w, gate, up, gate_held, up_held, gate_sum, up_sum, sems):
    depth, shard = gate_held.shape[1:]
    columns = columns_of(place[0], shard)
    here = [pl.ds(k * depth, depth) for k in range(parts)]
    gate_in = copies([gate_w.at[h, columns] for h in here], gate_held, sems.at[0])
    up_in = copies([up_w.at[h, columns] for h in here], up_held, sems.at[1])
    start(gate_in, up_in)
    for k in range(parts):
        part = rows[:, k * depth : (k + 1) * depth]
        gate_in[k].wait()
        up_in[k].wait()
        values = matmul(part, gate_held[k]), matmul(part, up_held[k])
        for value, total, out in zip(values, (gate_sum, up_sum), (gate, up)):
            if k:
                value += total[...]
            if k < parts - 1:
                total[...] = value
            else:
                out[...] = value.astype(out.dtype)


def partial_pre(place, rows, gate_w, up_w, shard, dtype):
    tokens, depth = rows.shape
    parts = depth // block_of(depth, 512)
    held = pltpu.VMEM((parts, depth // parts, shard), BF16)
    return pl.pallas_call(
        functools.partial(pre_body, parts),
        in_specs=[number(), whole(), in_hbm(), in_hbm()],
        out_specs=[whole()] * 2,
        out_shape=[jax.ShapeDtypeStruct((tokens, shard), dtype)] * 2,
        scratch_shapes=[held, held]
        + [pltpu.VMEM((tokens, shard), F32)] * 2
        + [pltpu.SemaphoreType.DMA((2, parts))],
        cost_estimate=cost(4 * tokens * depth * shard, 4 * depth * shard),
        compiler_params=params(),
        name="partial_pre",
    )(place, rows, gate_w, up_w)


def grad_body(count, places, rows, down_w, *rest):
    totals, (held, rows_t, sems) = rest[:count], rest[count:]
    shard = held.shape[1]
    loads = copies(
        [down_w.at[pl.ds(pl.multiple_of(places[j] * shard, LANES), shard)] for j in range(count)], held, sems
    )
    start(loads)
    rows_t[...] = rows[...].T
    half = shard // 2
    for j in range(count):
        loads[j].wait()
        low, high = matmul(held[j, :half], rows_t[...]), matmul(held[j, half:], rows_t[...])
        totals[j][...] = jnp.concatenate([low, high], axis=0).T


def partial_hidden_grad(places, rows, down_w, shard):
    count, (tokens, depth) = places.shape[0], rows.shape
    return list(
        pl.pallas_call(
            functools.partial(grad_body, count),
            in_specs=[number(), whole(), in_hbm()],
            out_specs=[whole()] * count,
            out_shape=[jax.ShapeDtypeStruct((tokens, shard), F32)] * count,
            scratch_shapes=[
                pltpu.VMEM((count, shard, depth), BF16),
                pltpu.VMEM((depth, tokens), BF16),
                pltpu.SemaphoreType.DMA((count,)),
            ],
            cost_estimate=cost(2 * count * tokens * depth * shard, 2 * count * depth * shard),
            compiler_params=params(),
            name="partial_hidden_grad",
        )(places, rows, down_w)
    )


def down_body(parts, first, place, hidden, down_w, rows, *rest):
    total, grad, held, made, hidden_t, in_sems, out_sems = rest[-7:]
    shard, step = held.shape[1:]
    units = columns_of(place[0], shard)
    here = [pl.ds(k * step, step) for k in range(parts)]
    loads = copies([down_w.at[units, h] for h in here], held, in_sems)
    start(loads)
    hidden_t[...] = hidden[...].T
    stores = []
    for k in range(parts):
        span = slice(k * step, (k + 1) * step)
        made[k] = matmul(hidden_t[...], rows[:, span]).astype(BF16)
        stores.append(pltpu.make_async_copy(made.at[k], grad.at[units, here[k]], out_sems.at[k]))
        stores[k].start()
        loads[k].wait()
        value = matmul(hidden[...], held[k])
        total[:, span] = value if first else rest[0][:, span] + value
    for store in stores:
        store.wait()


def down_shard(place, hidden, down_w, rows, before):
    tokens, shard = hidden.shape
    units, depth = down_w.shape
    step = block_of(depth, 512)
    parts = depth // step
    first = before is None
    held = pltpu.VMEM((parts, shard, step), BF16)
    return list(
        pl.pallas_call(
            functools.partial(down_body, parts, first),
            in_specs=[number(), whole(), in_hbm(), whole()] + ([] if first else [whole(), in_hbm()]),
            out_specs=[whole(), in_hbm()],
            out_shape=[
                jax.ShapeDtypeStruct((tokens, depth), F32),
                jax.ShapeDtypeStruct((units, depth), BF16),
            ],
            scratch_shapes=[held, held, pltpu.VMEM((shard, tokens), BF16)] + [pltpu.SemaphoreType.DMA((parts,))] * 2,
            input_output_aliases={} if first else {4: 0, 5: 1},
            cost_estimate=cost(4 * tokens * depth * shard, 4 * depth * shard),
            compiler_params=params(),
            name="down_shard",
        )(place, hidden, down_w, rows, *([] if first else before))
    )


def turn_body(source, out):
    out[...] = source[...].T


def turn(source):
    rows, cols = source.shape
    return pl.pallas_call(
        turn_body,
        in_specs=[whole()],
        out_specs=whole(),
        out_shape=jax.ShapeDtypeStruct((cols, rows), source.dtype),
        cost_estimate=cost(0, 4 * source.size),
        compiler_params=params(),
        name="turn",
    )(source)


def both_body(parts, first, reads, writes, place, pre, *rest):
    rest = list(rest)
    sources = [rest.pop(0) for _ in range(2)] if reads else []
    rows_t = rest.pop(0) if writes else None
    before = rest.pop(0) if reads and not first else None
    if writes and not first:
        del rest[:2]
    total = rest.pop(0) if reads else None
    grads = [rest.pop(0) for _ in range(2)] if writes else []
    if reads:
        held, turned, in_sems = rest[:3]
        del rest[:3]
    if writes:
        made, out_sems = rest
    buffer = held if reads else made
    step, shard = buffer.shape[1], buffer.shape[2] // 2
    half, columns = step // 2, columns_of(place[0], shard)
    here = [pl.ds(k * step, step) for k in range(parts)]
    sides = pl.ds(0, shard), pl.ds(shard, shard)
    loads = [
        [
            pltpu.make_async_copy(source.at[h, columns], held.at[k, :, sides[n]], in_sems.at[n, k])
            for n, source in enumerate(sources)
        ]
        for k, h in enumerate(here)
    ]
    start(*zip(*loads))
    if reads:
        turned[...] = pre[...].T
    stores = []
    for k in range(parts):
        span = slice(k * step, (k + 1) * step)
        if writes:
            low, high = (matmul(rows_t[pl.ds(k * step + n * half, half)], pre[...]) for n in range(2))
            made[k, :half] = low.astype(BF16)
            made[k, half:] = high.astype(BF16)
            for n in range(2):
                stores.append(
                    pltpu.make_async_copy(made.at[k, :, sides[n]], grads[n].at[here[k], columns], out_sems.at[n, k])
                )
                stores[-1].start()
        if reads:
            for copy in loads[k]:
                copy.wait()
            low, high = matmul(held[k, :half], turned[...]), matmul(held[k, half:], turned[...])
            value = jnp.concatenate([low, high], axis=0).T
            total[:, span] = value if first else before[:, span] + value
    for store in stores:
        store.wait()


def input_and_weights(place, pre, gate_w, up_w, rows_t, total, grads, reads=True, writes=True):
    tokens, shard = pre.shape[0], pre.shape[1] // 2
    depth, units = gate_w.shape
    step = block_of(depth, 512)
    parts = depth // step
    first = total is None
    operands, in_specs, out_specs, out_shape, aliases = [place, pre], [number(), whole()], [], [], {}
    held = pltpu.VMEM((parts, step, 2 * shard), BF16)
    scratch = []
    if reads:
        operands += [gate_w, up_w]
        in_specs += [in_hbm()] * 2
        out_specs += [whole()]
        out_shape += [jax.ShapeDtypeStruct((tokens, depth), F32)]
        scratch += [held, pltpu.VMEM((2 * shard, tokens), BF16), pltpu.SemaphoreType.DMA((2, parts))]
    if writes:
        operands += [rows_t]
        in_specs += [whole()]
        out_specs += [in_hbm()] * 2
        out_shape += [jax.ShapeDtypeStruct((depth, units), BF16)] * 2
        scratch += [held, pltpu.SemaphoreType.DMA((2, parts))]
    if reads and not first:
        aliases[len(operands)] = 0
        operands += [total]
        in_specs += [whole()]
    if writes and not first:
        aliases.update({len(operands) + n: len(out_shape) - 2 + n for n in range(2)})
        operands += grads
        in_specs += [in_hbm()] * 2
    got = list(
        pl.pallas_call(
            functools.partial(both_body, parts, first, reads, writes),
            in_specs=in_specs,
            out_specs=out_specs,
            out_shape=out_shape,
            scratch_shapes=scratch,
            input_output_aliases=aliases,
            cost_estimate=cost(4 * (reads + writes) * tokens * depth * shard, 4 * (reads + writes) * depth * shard),
            compiler_params=params(),
            name="_".join(["input"] * reads + ["weights"] * writes),
        )(*operands)
    )
    return got.pop(0) if reads else total, got if writes else grads


def shards(loop, width, inputs, gate_weight, up_weight, down_weight, out_grad):
    hidden_dev = gate_weight.shape[1]
    shard = hidden_dev // width
    chips = loop // 2
    own_rows = inputs.shape[0]

    z_perm = ring_perm(width)
    y_perm = [(2 * a + core, 2 * b + core) for a, b in ring_perm(chips) for core in (0, 1)]
    core_perm = [(k, k ^ 1) for k in range(loop)]

    def gather_core(mine):
        return jnp.concatenate(mine + [lax.ppermute(m, "loop", core_perm) for m in mine], axis=0)

    def scatter_chips(mine):
        slots = [mine[k * own_rows : (k + 1) * own_rows] for k in range(chips)]
        return ring_scatter(slots, "loop", y_perm, chips).astype(BF16)

    def scatter_core(total):
        half = chips * own_rows
        return total[:half] + lax.ppermute(total[half:], "loop", core_perm)

    place = ring_place(lax.axis_index("width"), width)
    places = lax.rem(place + width - jnp.arange(width, dtype=jnp.int32), jnp.int32(width))

    def hop(sent):
        return lax.ppermute(sent, "width", z_perm)

    def add(got, term):
        return got.astype(F32) + term

    def slot_of(array, slot):
        return lax.dynamic_slice_in_dim(array, places[slot] * shard, shard, axis=1)

    def pre_of(slot, rows):
        return partial_pre(places[slot : slot + 1], rows, gate_weight, up_weight, shard, F32)

    gate_held, up_held = load(places[1:2], gate_weight, up_weight, shard)
    mine = ring_gather(inputs, "loop", y_perm, chips)
    out_grad, mine[-1] = together(out_grad, mine[-1])
    gathered = gather_core(mine)
    gate_first, up_first = matmul(gathered, gate_held).astype(BF16), matmul(gathered, up_held).astype(BF16)
    gate, up = hop(gate_first), hop(up_first)
    rows, gate_first, up_first = together(gathered, gate_first, up_first)
    slots = [(k + 1) % width for k in range(width)]
    terms = [None] * width
    terms[slots[1]] = pre_of(slots[1], rows)
    piece = gather_core(ring_gather(out_grad, "loop", y_perm, chips))
    piece, *terms[slots[1]] = together(piece, *terms[slots[1]])
    grad_n = {1: partial_hidden_grad(places[1:2], piece, down_weight, shard)[0]}
    gate, up = add(gate, terms[slots[1]][0]).astype(BF16), add(up, terms[slots[1]][1]).astype(BF16)
    if width > 2:
        rows, piece, gate, up = together(rows, piece, gate, up)
    for slot in slots[2:3]:
        terms[slot] = pre_of(slot, rows)
        piece, *terms[slot] = together(piece, *terms[slot])
    order = jnp.concatenate([places[2:], places[:1]])
    grad_n.update(zip(slots[1:], partial_hidden_grad(order, piece, down_weight, shard)))
    rows, grad_n[slots[1]] = together(rows, grad_n[slots[1]])
    for slot in slots[3:]:
        terms[slot] = pre_of(slot, rows)

    sent = grad_n[1].astype(BF16)
    for h in range(1, width - 1):
        got = hop(sent)
        gate, up = hop(gate), hop(up)
        if h < width - 2:
            gate, up = add(gate, terms[slots[h + 1]][0]).astype(BF16), add(up, terms[slots[h + 1]][1]).astype(BF16)
        sent = add(got, grad_n[h + 1]).astype(BF16)
    gate, up = add(gate, terms[0][0]), add(up, terms[0][1])
    sig = jax.nn.sigmoid(gate)
    sent, hidden_own = together(sent, (gate * sig * up).astype(BF16))
    hidden_grad = add(hop(sent), grad_n[0])
    hidden = [hidden_own, hop(hidden_own)]

    rows_t = turn(gathered)
    down = down_shard(places[:1], hidden[0], down_weight, piece, None)
    pre_gate = (hidden_grad * up * sig * (1.0 + gate * (1.0 - sig))).astype(BF16)
    pre_up = (hidden_grad * gate * sig).astype(BF16)
    pre = [jnp.concatenate([pre_gate, pre_up], axis=1)]
    pre[0], down[0], hidden[1] = together(pre[0], down[0], hidden[1])
    weights = gate_weight, up_weight, rows_t
    total, grads = None, None
    for k in range(width - 1):
        pre.append(hop(pre[k]))
        if k < width - 2:
            hidden.append(hop(hidden[k + 1]))
        total, grads = input_and_weights(places[k : k + 1], pre[k], *weights, total, grads)
        down = down_shard(places[k + 1 : k + 2], hidden[k + 1], down_weight, piece, down)
        if k < width - 2:
            pre[k + 1], total, down[0], hidden[k + 2] = together(pre[k + 1], total, down[0], hidden[k + 2])
    here = places[width - 1 :]
    pre[-1], total, down[0] = together(pre[-1], total, down[0])
    output_mine = scatter_core(down[0])
    total, _ = input_and_weights(here, pre[-1], *weights, total, grads, writes=False)
    input_mine = scatter_core(total)
    pre[-1], total, output_mine = together(pre[-1], total, output_mine)
    output = scatter_chips(output_mine)
    _, (gate_grad, up_grad) = input_and_weights(here, pre[-1], *weights, total, grads, reads=False)
    input_grad = scatter_chips(input_mine)
    down_grad = down[1]
    return (output, input_grad, gate_grad, up_grad, down_grad)


def plain(inputs, gate_weight, up_weight, down_weight, out_grad):
    gathered = lax.all_gather(inputs, "loop", axis=0, tiled=True)
    gate = lax.psum(matmul(gathered, gate_weight), "width")
    up = lax.psum(matmul(gathered, up_weight), "width")
    sig = jax.nn.sigmoid(gate)
    hidden = (gate * sig * up).astype(BF16)
    output = lax.psum_scatter(matmul(hidden, down_weight), "loop", scatter_dimension=0, tiled=True).astype(BF16)
    piece = lax.all_gather(out_grad, "loop", axis=0, tiled=True)
    down_grad = contract_rows(hidden, piece).astype(BF16)
    hidden_grad = lax.psum(contract_cols(piece, down_weight), "width")
    pre_gate = (hidden_grad * up * sig * (1.0 + gate * (1.0 - sig))).astype(BF16)
    pre_up = (hidden_grad * gate * sig).astype(BF16)
    input_grad = lax.psum_scatter(
        contract_cols(pre_gate, gate_weight) + contract_cols(pre_up, up_weight),
        "loop",
        scatter_dimension=0,
        tiled=True,
    ).astype(BF16)
    gate_grad = contract_rows(gathered, pre_gate).astype(BF16)
    up_grad = contract_rows(gathered, pre_up).astype(BF16)
    return (output, input_grad, gate_grad, up_grad, down_grad)


def solution(mesh):
    loop, width = mesh.shape["loop"], mesh.shape["width"]

    def layer(*arrays):
        units = arrays[1].shape[1]
        if units % (width * LANES) or loop % 2 or width < 2:
            return plain(*arrays)
        return shards(loop, width, *arrays)

    in_specs = (
        P(("groups", "loop"), "width"),
        P("width", "loop"),
        P("width", "loop"),
        P("loop", "width"),
        P(("groups", "loop"), "width"),
    )
    out_specs = (
        P(("groups", "loop"), "width"),
        P(("groups", "loop"), "width"),
        P(("groups", "width"), "loop"),
        P(("groups", "width"), "loop"),
        P(("groups", "loop"), "width"),
    )
    return jax.shard_map(layer, mesh=mesh, in_specs=in_specs, out_specs=out_specs, check_vma=False)
```

```python
import functools

import jax
import jax.numpy as jnp
from jax import lax
from jax.experimental import pallas as pl
from jax.experimental.pallas import tpu as pltpu
from jax.sharding import PartitionSpec as P

BF16 = jnp.bfloat16
F32 = jnp.float32
LANES = 128
MIB = 1024 * 1024
PART = 512
KERNEL_VMEM = 46 * MIB


def contract_rows(left, right):
    return lax.dot_general(left, right, (((0,), (0,)), ((), ())), preferred_element_type=F32)


def contract_cols(left, right):
    return lax.dot_general(left, right, (((1,), (1,)), ((), ())), preferred_element_type=F32)


def matmul(left, right):
    return jnp.dot(left, right, preferred_element_type=F32)


def block_of(size, most):
    return max(b for b in range(LANES, most + 1, LANES) if size % b == 0)


def ring_order(n):
    return [0] + list(range(1, n, 2)) + [k for k in range(n - 1, 1, -1) if k % 2 == 0]


def ring_perm(n):
    order = ring_order(n)
    return [(order[k], order[(k + 1) % n]) for k in range(n)]


def ring_place(index, n):
    order = ring_order(n)
    place = jnp.int32(0)
    for k in range(n):
        place = jnp.where(index == order[k], k, place)
    return place.astype(jnp.int32)


def ring_gather(own, axis, perm, n):
    slots = [own]
    for _ in range(n - 1):
        slots.append(lax.ppermute(slots[-1], axis, perm))
    return slots


def ring_scatter(slots, axis, perm, n):
    total = slots[1 % n]
    for h in range(1, n):
        got = lax.ppermute(total.astype(BF16), axis, perm)
        total = got.astype(F32) + slots[(h + 1) % n]
    return total


def together(*arrays):
    return lax.optimization_barrier(list(arrays))


def params():
    return pltpu.CompilerParams(vmem_limit_bytes=KERNEL_VMEM)


def cost(flops, moved):
    return pl.CostEstimate(flops=flops // 64, bytes_accessed=moved // 64, transcendentals=0)


def whole():
    return pl.BlockSpec(memory_space=pltpu.VMEM)


def in_hbm():
    return pl.BlockSpec(memory_space=pltpu.HBM)


def number():
    return pl.BlockSpec(memory_space=pltpu.SMEM)


def copies(blocks, held, sems):
    return [pltpu.make_async_copy(block, held.at[k], sems.at[k]) for k, block in enumerate(blocks)]


def start(*lists):
    for group in zip(*lists):
        for copy in group:
            copy.start()


def columns_of(place, shard):
    return pl.ds(pl.multiple_of(place * shard, LANES), shard)


def load_body(parts, place, gate_w, up_w, gate_held, up_held, sems):
    depth, shard = gate_held.shape
    step, columns = depth // parts, columns_of(place[0], shard)
    loads = []
    for n, (source, held) in enumerate(((gate_w, gate_held), (up_w, up_held))):
        for k in range(parts):
            here = pl.ds(k * step, step)
            loads.append(pltpu.make_async_copy(source.at[here, columns], held.at[here], sems.at[n, k]))
            loads[-1].start()
    for copy in loads:
        copy.wait()


def load(place, gate_w, up_w, shard):
    parts, depth = 4, gate_w.shape[0]
    return pl.pallas_call(
        functools.partial(load_body, parts),
        in_specs=[number(), in_hbm(), in_hbm()],
        out_specs=[whole()] * 2,
        out_shape=[jax.ShapeDtypeStruct((depth, shard), gate_w.dtype)] * 2,
        scratch_shapes=[pltpu.SemaphoreType.DMA((2, parts))],
        cost_estimate=cost(0, 4 * depth * shard),
        compiler_params=params(),
        name="load",
    )(place, gate_w, up_w)


def pre_body(parts, place, rows, gate_w, up_w, gate, up, gate_held, up_held, gate_sum, up_sum, sems):
    depth, shard = gate_held.shape[1:]
    columns = columns_of(place[0], shard)
    here = [pl.ds(k * depth, depth) for k in range(parts)]
    gate_in = copies([gate_w.at[h, columns] for h in here], gate_held, sems.at[0])
    up_in = copies([up_w.at[h, columns] for h in here], up_held, sems.at[1])
    start(gate_in, up_in)
    for k in range(parts):
        part = rows[:, k * depth : (k + 1) * depth]
        gate_in[k].wait()
        up_in[k].wait()
        values = matmul(part, gate_held[k]), matmul(part, up_held[k])
        for value, total, out in zip(values, (gate_sum, up_sum), (gate, up)):
            if k:
                value += total[...]
            if k < parts - 1:
                total[...] = value
            else:
                out[...] = value.astype(out.dtype)


def partial_pre(place, rows, gate_w, up_w, shard, dtype):
    tokens, depth = rows.shape
    parts = depth // block_of(depth, PART)
    held = pltpu.VMEM((parts, depth // parts, shard), BF16)
    return pl.pallas_call(
        functools.partial(pre_body, parts),
        in_specs=[number(), whole(), in_hbm(), in_hbm()],
        out_specs=[whole()] * 2,
        out_shape=[jax.ShapeDtypeStruct((tokens, shard), dtype)] * 2,
        scratch_shapes=[held, held]
        + [pltpu.VMEM((tokens, shard), F32)] * 2
        + [pltpu.SemaphoreType.DMA((2, parts))],
        cost_estimate=cost(4 * tokens * depth * shard, 4 * depth * shard),
        compiler_params=params(),
        name="partial_pre",
    )(place, rows, gate_w, up_w)


def grad_body(count, places, rows, down_w, *rest):
    totals, (held, rows_t, sems) = rest[:count], rest[count:]
    shard = held.shape[1]
    loads = copies(
        [down_w.at[pl.ds(pl.multiple_of(places[j] * shard, LANES), shard)] for j in range(count)], held, sems
    )
    start(loads)
    rows_t[...] = rows[...].T
    half = shard // 2
    for j in range(count):
        loads[j].wait()
        low, high = matmul(held[j, :half], rows_t[...]), matmul(held[j, half:], rows_t[...])
        totals[j][...] = jnp.concatenate([low, high], axis=0).T


def partial_hidden_grad(places, rows, down_w, shard):
    count, (tokens, depth) = places.shape[0], rows.shape
    return list(
        pl.pallas_call(
            functools.partial(grad_body, count),
            in_specs=[number(), whole(), in_hbm()],
            out_specs=[whole()] * count,
            out_shape=[jax.ShapeDtypeStruct((tokens, shard), F32)] * count,
            scratch_shapes=[
                pltpu.VMEM((count, shard, depth), BF16),
                pltpu.VMEM((depth, tokens), BF16),
                pltpu.SemaphoreType.DMA((count,)),
            ],
            cost_estimate=cost(2 * count * tokens * depth * shard, 2 * count * depth * shard),
            compiler_params=params(),
            name="partial_hidden_grad",
        )(places, rows, down_w)
    )


def down_body(parts, first, place, hidden, down_w, rows, *rest):
    total, grad, held, made, hidden_t, in_sems, out_sems = rest[-7:]
    shard, step = held.shape[1:]
    units = columns_of(place[0], shard)
    here = [pl.ds(k * step, step) for k in range(parts)]
    loads = copies([down_w.at[units, h] for h in here], held, in_sems)
    start(loads)
    hidden_t[...] = hidden[...].T
    stores = []
    for k in range(parts):
        span = slice(k * step, (k + 1) * step)
        made[k] = matmul(hidden_t[...], rows[:, span]).astype(BF16)
        stores.append(pltpu.make_async_copy(made.at[k], grad.at[units, here[k]], out_sems.at[k]))
        stores[k].start()
        loads[k].wait()
        value = matmul(hidden[...], held[k])
        total[:, span] = value if first else rest[0][:, span] + value
    for store in stores:
        store.wait()


def down_shard(place, hidden, down_w, rows, before):
    tokens, shard = hidden.shape
    units, depth = down_w.shape
    step = block_of(depth, PART)
    parts = depth // step
    first = before is None
    held = pltpu.VMEM((parts, shard, step), BF16)
    return list(
        pl.pallas_call(
            functools.partial(down_body, parts, first),
            in_specs=[number(), whole(), in_hbm(), whole()] + ([] if first else [whole(), in_hbm()]),
            out_specs=[whole(), in_hbm()],
            out_shape=[
                jax.ShapeDtypeStruct((tokens, depth), F32),
                jax.ShapeDtypeStruct((units, depth), BF16),
            ],
            scratch_shapes=[held, held, pltpu.VMEM((shard, tokens), BF16)] + [pltpu.SemaphoreType.DMA((parts,))] * 2,
            input_output_aliases={} if first else {4: 0, 5: 1},
            cost_estimate=cost(4 * tokens * depth * shard, 4 * depth * shard),
            compiler_params=params(),
            name="down_shard",
        )(place, hidden, down_w, rows, *([] if first else before))
    )


def turn_body(source, out):
    out[...] = source[...].T


def turn(source):
    rows, cols = source.shape
    return pl.pallas_call(
        turn_body,
        in_specs=[whole()],
        out_specs=whole(),
        out_shape=jax.ShapeDtypeStruct((cols, rows), source.dtype),
        cost_estimate=cost(0, 4 * source.size),
        compiler_params=params(),
        name="turn",
    )(source)


def both_body(parts, span, first, reads, writes, place, pre, *rest):
    rest = list(rest)
    sources = [rest.pop(0) for _ in range(2)] if reads else []
    rows_t = rest.pop(0) if writes else None
    before = rest.pop(0) if reads and not first else None
    if writes and not first:
        del rest[:2]
    total = rest.pop(0) if reads else None
    grads = [rest.pop(0) for _ in range(2)] if writes else []
    if reads:
        held, turned, in_sems = rest[:3]
        del rest[:3]
    if writes:
        made, out_sems = rest
    buffer = held if reads else made
    step, shard = buffer.shape[1], buffer.shape[2] // 2
    half, columns = step // 2, columns_of(place[0], shard)
    here = [pl.ds(k * step, step) for k in range(parts)]
    sides = pl.ds(0, shard), pl.ds(shard, shard)
    loads = [
        [
            pltpu.make_async_copy(source.at[h, columns], held.at[k, :, sides[n]], in_sems.at[n, k])
            for n, source in enumerate(sources)
        ]
        for k, h in list(enumerate(here))[slice(*span)]
    ]
    start(*zip(*loads))
    if reads:
        turned[...] = pre[...].T
    stores = []
    for k in range(*span):
        strip = slice(k * step, (k + 1) * step)
        if writes:
            low, high = (matmul(rows_t[pl.ds(k * step + n * half, half)], pre[...]) for n in range(2))
            made[k, :half] = low.astype(BF16)
            made[k, half:] = high.astype(BF16)
            for n in range(2):
                stores.append(
                    pltpu.make_async_copy(made.at[k, :, sides[n]], grads[n].at[here[k], columns], out_sems.at[n, k])
                )
                stores[-1].start()
        if reads:
            for copy in loads[k - span[0]]:
                copy.wait()
            low, high = matmul(held[k, :half], turned[...]), matmul(held[k, half:], turned[...])
            value = jnp.concatenate([low, high], axis=0).T
            made_here = slice((k - span[0]) * step, (k - span[0] + 1) * step)
            total[:, made_here] = value if first else before[:, strip] + value
    for store in stores:
        store.wait()


def input_and_weights(place, pre, gate_w, up_w, rows_t, total, grads, reads=True, writes=True, share=(0, 1)):
    tokens, shard = pre.shape[0], pre.shape[1] // 2
    depth, units = gate_w.shape
    step = block_of(depth, PART)
    parts = depth // step
    first = total is None
    span = tuple(parts * n // share[1] for n in (share[0], share[0] + 1))
    operands, in_specs, out_specs, out_shape, aliases = [place, pre], [number(), whole()], [], [], {}
    held = pltpu.VMEM((parts, step, 2 * shard), BF16)
    scratch = []
    if reads:
        operands += [gate_w, up_w]
        in_specs += [in_hbm()] * 2
        out_specs += [whole()]
        out_shape += [jax.ShapeDtypeStruct((tokens, depth // share[1]), F32)]
        scratch += [held, pltpu.VMEM((2 * shard, tokens), BF16), pltpu.SemaphoreType.DMA((2, parts))]
    if writes:
        operands += [rows_t]
        in_specs += [whole()]
        out_specs += [in_hbm()] * 2
        out_shape += [jax.ShapeDtypeStruct((depth, units), BF16)] * 2
        scratch += [held, pltpu.SemaphoreType.DMA((2, parts))]
    if reads and not first:
        if share[1] == 1:
            aliases[len(operands)] = 0
        operands += [total]
        in_specs += [whole()]
    if writes and not first:
        aliases.update({len(operands) + n: len(out_shape) - 2 + n for n in range(2)})
        operands += grads
        in_specs += [in_hbm()] * 2
    got = list(
        pl.pallas_call(
            functools.partial(both_body, parts, span, first, reads, writes),
            in_specs=in_specs,
            out_specs=out_specs,
            out_shape=out_shape,
            scratch_shapes=scratch,
            input_output_aliases=aliases,
            cost_estimate=cost(4 * (reads + writes) * tokens * depth * shard, 4 * (reads + writes) * depth * shard),
            compiler_params=params(),
            name="_".join(["input"] * reads + ["weights"] * writes),
        )(*operands)
    )
    return got.pop(0) if reads else total, got if writes else grads


def shards(loop, width, inputs, gate_weight, up_weight, down_weight, out_grad):
    hidden_dev = gate_weight.shape[1]
    shard = hidden_dev // width
    chips = loop // 2
    own_rows = inputs.shape[0]

    z_perm = ring_perm(width)
    y_perm = [(2 * a + core, 2 * b + core) for a, b in ring_perm(chips) for core in (0, 1)]
    core_perm = [(k, k ^ 1) for k in range(loop)]

    def gather_core(mine):
        return jnp.concatenate(mine + [lax.ppermute(m, "loop", core_perm) for m in mine], axis=0)

    def scatter_chips(mine):
        slots = [mine[k * own_rows : (k + 1) * own_rows] for k in range(chips)]
        return ring_scatter(slots, "loop", y_perm, chips).astype(BF16)

    def scatter_core(total):
        half = chips * own_rows
        return total[:half] + lax.ppermute(total[half:], "loop", core_perm)

    place = ring_place(lax.axis_index("width"), width)
    places = lax.rem(place + width - jnp.arange(width, dtype=jnp.int32), jnp.int32(width))

    def hop(sent):
        return lax.ppermute(sent, "width", z_perm)

    def add(got, term):
        return got.astype(F32) + term

    def slot_of(array, slot):
        return lax.dynamic_slice_in_dim(array, places[slot] * shard, shard, axis=1)

    def pre_of(slot, rows):
        return partial_pre(places[slot : slot + 1], rows, gate_weight, up_weight, shard, F32)

    gate_held, up_held = load(places[1:2], gate_weight, up_weight, shard)
    mine = ring_gather(inputs, "loop", y_perm, chips)
    out_grad, mine[-1] = together(out_grad, mine[-1])
    gathered = gather_core(mine)
    gate_first, up_first = matmul(gathered, gate_held).astype(BF16), matmul(gathered, up_held).astype(BF16)
    gate, up = hop(gate_first), hop(up_first)
    rows, gate_first, up_first = together(gathered, gate_first, up_first)
    slots = [(k + 1) % width for k in range(width)]
    terms = [None] * width
    terms[slots[1]] = pre_of(slots[1], rows)
    piece = gather_core(ring_gather(out_grad, "loop", y_perm, chips))
    piece, *terms[slots[1]] = together(piece, *terms[slots[1]])
    grad_n = {1: partial_hidden_grad(places[1:2], piece, down_weight, shard)[0]}
    gate, up = add(gate, terms[slots[1]][0]).astype(BF16), add(up, terms[slots[1]][1]).astype(BF16)
    if width > 2:
        rows, piece, gate, up = together(rows, piece, gate, up)
    for slot in slots[2:3]:
        terms[slot] = pre_of(slot, rows)
        piece, *terms[slot] = together(piece, *terms[slot])
    order = jnp.concatenate([places[2:], places[:1]])
    grad_n.update(zip(slots[1:], partial_hidden_grad(order, piece, down_weight, shard)))
    rows, grad_n[slots[1]] = together(rows, grad_n[slots[1]])
    for slot in slots[3:]:
        terms[slot] = pre_of(slot, rows)

    sent = grad_n[1].astype(BF16)
    for h in range(1, width - 1):
        got = hop(sent)
        gate, up = hop(gate), hop(up)
        if h < width - 2:
            gate, up = add(gate, terms[slots[h + 1]][0]).astype(BF16), add(up, terms[slots[h + 1]][1]).astype(BF16)
        sent = add(got, grad_n[h + 1]).astype(BF16)
    gate, up = add(gate, terms[0][0]), add(up, terms[0][1])
    sig = jax.nn.sigmoid(gate)
    sent, hidden_own = together(sent, (gate * sig * up).astype(BF16))
    hidden_grad = add(hop(sent), grad_n[0])
    hidden = [hidden_own, hop(hidden_own)]

    rows_t = turn(gathered)
    down = down_shard(places[:1], hidden[0], down_weight, piece, None)
    pre_gate = (hidden_grad * up * sig * (1.0 + gate * (1.0 - sig))).astype(BF16)
    pre_up = (hidden_grad * gate * sig).astype(BF16)
    pre = [jnp.concatenate([pre_gate, pre_up], axis=1)]
    pre[0], down[0], hidden[1] = together(pre[0], down[0], hidden[1])
    weights = gate_weight, up_weight, rows_t
    total, grads = None, None
    for k in range(width - 1):
        pre.append(hop(pre[k]))
        total, grads = input_and_weights(places[k : k + 1], pre[k], *weights, total, grads)
        if k < width - 2:
            hidden[k + 1], total = together(hidden[k + 1], total)
            hidden.append(hop(hidden[k + 1]))
        down = down_shard(places[k + 1 : k + 2], hidden[k + 1], down_weight, piece, down)
        if k < width - 2:
            pre[k + 1], total, down[0], hidden[k + 2] = together(pre[k + 1], total, down[0], hidden[k + 2])
    here = places[width - 1 :]
    pre[-1], total, down[0] = together(pre[-1], total, down[0])
    output_mine = scatter_core(down[0])
    shares, last = 1 if inputs.shape[1] % (2 * PART) else 2, pre[-1]
    mines = []
    for n in range(shares):
        part, _ = input_and_weights(here, last, *weights, total, grads, writes=False, share=(n, shares))
        if n == 0:
            part, last, output_mine = together(part, last, output_mine)
            output = scatter_chips(output_mine)
        if n == shares - 1:
            part, output = together(part, output)
        mines.append(scatter_core(part))
        last, part = together(last, part)
    _, (gate_grad, up_grad) = input_and_weights(here, last, *weights, total, grads, reads=False)
    input_grad = scatter_chips(jnp.concatenate(mines, axis=1))
    down_grad = down[1]
    return (output, input_grad, gate_grad, up_grad, down_grad)


def plain(inputs, gate_weight, up_weight, down_weight, out_grad):
    gathered = lax.all_gather(inputs, "loop", axis=0, tiled=True)
    gate = lax.psum(matmul(gathered, gate_weight), "width")
    up = lax.psum(matmul(gathered, up_weight), "width")
    sig = jax.nn.sigmoid(gate)
    hidden = (gate * sig * up).astype(BF16)
    output = lax.psum_scatter(matmul(hidden, down_weight), "loop", scatter_dimension=0, tiled=True).astype(BF16)
    piece = lax.all_gather(out_grad, "loop", axis=0, tiled=True)
    down_grad = contract_rows(hidden, piece).astype(BF16)
    hidden_grad = lax.psum(contract_cols(piece, down_weight), "width")
    pre_gate = (hidden_grad * up * sig * (1.0 + gate * (1.0 - sig))).astype(BF16)
    pre_up = (hidden_grad * gate * sig).astype(BF16)
    input_grad = lax.psum_scatter(
        contract_cols(pre_gate, gate_weight) + contract_cols(pre_up, up_weight),
        "loop",
        scatter_dimension=0,
        tiled=True,
    ).astype(BF16)
    gate_grad = contract_rows(gathered, pre_gate).astype(BF16)
    up_grad = contract_rows(gathered, pre_up).astype(BF16)
    return (output, input_grad, gate_grad, up_grad, down_grad)


def solution(mesh):
    loop, width = mesh.shape["loop"], mesh.shape["width"]

    def layer(*arrays):
        units = arrays[1].shape[1]
        if units % (width * LANES) or loop % 2 or width < 2:
            return plain(*arrays)
        return shards(loop, width, *arrays)

    in_specs = (
        P(("groups", "loop"), "width"),
        P("width", "loop"),
        P("width", "loop"),
        P("loop", "width"),
        P(("groups", "loop"), "width"),
    )
    out_specs = (
        P(("groups", "loop"), "width"),
        P(("groups", "loop"), "width"),
        P(("groups", "width"), "loop"),
        P(("groups", "width"), "loop"),
        P(("groups", "loop"), "width"),
    )
    return jax.shard_map(layer, mesh=mesh, in_specs=in_specs, out_specs=out_specs, check_vma=False)
```

```python
import functools

import jax
import jax.numpy as jnp
from jax import lax
from jax.experimental import pallas as pl
from jax.experimental.pallas import tpu as pltpu
from jax.sharding import PartitionSpec as P

BF16 = jnp.bfloat16
F32 = jnp.float32
LANES = 128
MIB = 1024 * 1024
PART = 512
KERNEL_VMEM = 46 * MIB


def contract_rows(left, right):
    return lax.dot_general(left, right, (((0,), (0,)), ((), ())), preferred_element_type=F32)


def contract_cols(left, right):
    return lax.dot_general(left, right, (((1,), (1,)), ((), ())), preferred_element_type=F32)


def matmul(left, right):
    return jnp.dot(left, right, preferred_element_type=F32)


def block_of(size, most):
    return max(b for b in range(LANES, most + 1, LANES) if size % b == 0)


def ring_order(n):
    return [0] + list(range(1, n, 2)) + [k for k in range(n - 1, 1, -1) if k % 2 == 0]


def ring_perm(n):
    order = ring_order(n)
    return [(order[k], order[(k + 1) % n]) for k in range(n)]


def ring_place(index, n):
    order = ring_order(n)
    place = jnp.int32(0)
    for k in range(n):
        place = jnp.where(index == order[k], k, place)
    return place.astype(jnp.int32)


def ring_gather(own, axis, perm, n):
    slots = [own]
    for _ in range(n - 1):
        slots.append(lax.ppermute(slots[-1], axis, perm))
    return slots


def ring_scatter(slots, axis, perm, n):
    total = slots[1 % n]
    for h in range(1, n):
        got = lax.ppermute(total.astype(BF16), axis, perm)
        total = got.astype(F32) + slots[(h + 1) % n]
    return total


def together(*arrays):
    return lax.optimization_barrier(list(arrays))


def params():
    return pltpu.CompilerParams(vmem_limit_bytes=KERNEL_VMEM)


def cost(flops, moved):
    return pl.CostEstimate(flops=flops // 64, bytes_accessed=moved // 64, transcendentals=0)


def whole():
    return pl.BlockSpec(memory_space=pltpu.VMEM)


def in_hbm():
    return pl.BlockSpec(memory_space=pltpu.HBM)


def number():
    return pl.BlockSpec(memory_space=pltpu.SMEM)


def copies(blocks, held, sems):
    return [pltpu.make_async_copy(block, held.at[k], sems.at[k]) for k, block in enumerate(blocks)]


def start(*lists):
    for group in zip(*lists):
        for copy in group:
            copy.start()


def columns_of(place, shard):
    return pl.ds(pl.multiple_of(place * shard, LANES), shard)


def load_body(parts, place, gate_w, up_w, gate_held, up_held, sems):
    depth, shard = gate_held.shape
    step, columns = depth // parts, columns_of(place[0], shard)
    loads = []
    for n, (source, held) in enumerate(((gate_w, gate_held), (up_w, up_held))):
        for k in range(parts):
            here = pl.ds(k * step, step)
            loads.append(pltpu.make_async_copy(source.at[here, columns], held.at[here], sems.at[n, k]))
            loads[-1].start()
    for copy in loads:
        copy.wait()


def load(place, gate_w, up_w, shard):
    parts, depth = 4, gate_w.shape[0]
    return pl.pallas_call(
        functools.partial(load_body, parts),
        in_specs=[number(), in_hbm(), in_hbm()],
        out_specs=[whole()] * 2,
        out_shape=[jax.ShapeDtypeStruct((depth, shard), gate_w.dtype)] * 2,
        scratch_shapes=[pltpu.SemaphoreType.DMA((2, parts))],
        cost_estimate=cost(0, 4 * depth * shard),
        compiler_params=params(),
        name="load",
    )(place, gate_w, up_w)


def pre_body(parts, place, rows, gate_w, up_w, gate, up, gate_held, up_held, gate_sum, up_sum, sems):
    depth, shard = gate_held.shape[1:]
    columns = columns_of(place[0], shard)
    here = [pl.ds(k * depth, depth) for k in range(parts)]
    gate_in = copies([gate_w.at[h, columns] for h in here], gate_held, sems.at[0])
    up_in = copies([up_w.at[h, columns] for h in here], up_held, sems.at[1])
    start(gate_in, up_in)
    for k in range(parts):
        part = rows[:, k * depth : (k + 1) * depth]
        gate_in[k].wait()
        up_in[k].wait()
        values = matmul(part, gate_held[k]), matmul(part, up_held[k])
        for value, total, out in zip(values, (gate_sum, up_sum), (gate, up)):
            if k:
                value += total[...]
            if k < parts - 1:
                total[...] = value
            else:
                out[...] = value.astype(out.dtype)


def partial_pre(place, rows, gate_w, up_w, shard, dtype):
    tokens, depth = rows.shape
    parts = depth // block_of(depth, PART)
    held = pltpu.VMEM((parts, depth // parts, shard), BF16)
    return pl.pallas_call(
        functools.partial(pre_body, parts),
        in_specs=[number(), whole(), in_hbm(), in_hbm()],
        out_specs=[whole()] * 2,
        out_shape=[jax.ShapeDtypeStruct((tokens, shard), dtype)] * 2,
        scratch_shapes=[held, held]
        + [pltpu.VMEM((tokens, shard), F32)] * 2
        + [pltpu.SemaphoreType.DMA((2, parts))],
        cost_estimate=cost(4 * tokens * depth * shard, 4 * depth * shard),
        compiler_params=params(),
        name="partial_pre",
    )(place, rows, gate_w, up_w)


def grad_body(count, places, rows, down_w, *rest):
    totals, (held, rows_t, sems) = rest[:count], rest[count:]
    shard = held.shape[1]
    loads = copies(
        [down_w.at[pl.ds(pl.multiple_of(places[j] * shard, LANES), shard)] for j in range(count)], held, sems
    )
    start(loads)
    rows_t[...] = rows[...].T
    half = shard // 2
    for j in range(count):
        loads[j].wait()
        low, high = matmul(held[j, :half], rows_t[...]), matmul(held[j, half:], rows_t[...])
        totals[j][...] = jnp.concatenate([low, high], axis=0).T


def partial_hidden_grad(places, rows, down_w, shard):
    count, (tokens, depth) = places.shape[0], rows.shape
    return list(
        pl.pallas_call(
            functools.partial(grad_body, count),
            in_specs=[number(), whole(), in_hbm()],
            out_specs=[whole()] * count,
            out_shape=[jax.ShapeDtypeStruct((tokens, shard), F32)] * count,
            scratch_shapes=[
                pltpu.VMEM((count, shard, depth), BF16),
                pltpu.VMEM((depth, tokens), BF16),
                pltpu.SemaphoreType.DMA((count,)),
            ],
            cost_estimate=cost(2 * count * tokens * depth * shard, 2 * count * depth * shard),
            compiler_params=params(),
            name="partial_hidden_grad",
        )(places, rows, down_w)
    )


def down_body(parts, first, place, hidden, down_w, rows, *rest):
    total, grad, held, made, hidden_t, in_sems, out_sems = rest[-7:]
    shard, step = held.shape[1:]
    units = columns_of(place[0], shard)
    here = [pl.ds(k * step, step) for k in range(parts)]
    loads = copies([down_w.at[units, h] for h in here], held, in_sems)
    start(loads)
    hidden_t[...] = hidden[...].T
    stores = []
    for k in range(parts):
        span = slice(k * step, (k + 1) * step)
        made[k] = matmul(hidden_t[...], rows[:, span]).astype(BF16)
        stores.append(pltpu.make_async_copy(made.at[k], grad.at[units, here[k]], out_sems.at[k]))
        stores[k].start()
        loads[k].wait()
        value = matmul(hidden[...], held[k])
        total[:, span] = value if first else rest[0][:, span] + value
    for store in stores:
        store.wait()


def down_shard(place, hidden, down_w, rows, before):
    tokens, shard = hidden.shape
    units, depth = down_w.shape
    step = block_of(depth, PART)
    parts = depth // step
    first = before is None
    held = pltpu.VMEM((parts, shard, step), BF16)
    return list(
        pl.pallas_call(
            functools.partial(down_body, parts, first),
            in_specs=[number(), whole(), in_hbm(), whole()] + ([] if first else [whole(), in_hbm()]),
            out_specs=[whole(), in_hbm()],
            out_shape=[
                jax.ShapeDtypeStruct((tokens, depth), F32),
                jax.ShapeDtypeStruct((units, depth), BF16),
            ],
            scratch_shapes=[held, held, pltpu.VMEM((shard, tokens), BF16)] + [pltpu.SemaphoreType.DMA((parts,))] * 2,
            input_output_aliases={} if first else {4: 0, 5: 1},
            cost_estimate=cost(4 * tokens * depth * shard, 4 * depth * shard),
            compiler_params=params(),
            name="down_shard",
        )(place, hidden, down_w, rows, *([] if first else before))
    )


def turn_body(source, out):
    out[...] = source[...].T


def turn(source):
    rows, cols = source.shape
    return pl.pallas_call(
        turn_body,
        in_specs=[whole()],
        out_specs=whole(),
        out_shape=jax.ShapeDtypeStruct((cols, rows), source.dtype),
        cost_estimate=cost(0, 4 * source.size),
        compiler_params=params(),
        name="turn",
    )(source)


def both_body(parts, first, reads, writes, place, pre, *rest):
    rest = list(rest)
    sources = [rest.pop(0) for _ in range(2)] if reads else []
    rows_t = rest.pop(0) if writes else None
    before = rest.pop(0) if reads and not first else None
    if writes and not first:
        del rest[:2]
    total = rest.pop(0) if reads else None
    grads = [rest.pop(0) for _ in range(2)] if writes else []
    if reads:
        held, turned, in_sems = rest[:3]
        del rest[:3]
    if writes:
        made, out_sems = rest
    buffer = held if reads else made
    step, shard = buffer.shape[1], buffer.shape[2] // 2
    half, columns = step // 2, columns_of(place[0], shard)
    here = [pl.ds(k * step, step) for k in range(parts)]
    sides = pl.ds(0, shard), pl.ds(shard, shard)
    loads = [
        [
            pltpu.make_async_copy(source.at[h, columns], held.at[k, :, sides[n]], in_sems.at[n, k])
            for n, source in enumerate(sources)
        ]
        for k, h in enumerate(here)
    ]
    start(*zip(*loads))
    if reads:
        turned[...] = pre[...].T
    stores = []
    for k in range(parts):
        strip = slice(k * step, (k + 1) * step)
        if writes:
            low, high = (matmul(rows_t[pl.ds(k * step + n * half, half)], pre[...]) for n in range(2))
            made[k, :half] = low.astype(BF16)
            made[k, half:] = high.astype(BF16)
            for n in range(2):
                stores.append(
                    pltpu.make_async_copy(made.at[k, :, sides[n]], grads[n].at[here[k], columns], out_sems.at[n, k])
                )
                stores[-1].start()
        if reads:
            for copy in loads[k]:
                copy.wait()
            low, high = matmul(held[k, :half], turned[...]), matmul(held[k, half:], turned[...])
            value = jnp.concatenate([low, high], axis=0).T
            total[:, strip] = value if first else before[:, strip] + value
    for store in stores:
        store.wait()


def input_and_weights(place, pre, gate_w, up_w, rows_t, total, grads, reads=True, writes=True):
    tokens, shard = pre.shape[0], pre.shape[1] // 2
    depth, units = gate_w.shape
    step = block_of(depth, PART)
    parts = depth // step
    first = total is None
    operands, in_specs, out_specs, out_shape, aliases = [place, pre], [number(), whole()], [], [], {}
    held = pltpu.VMEM((parts, step, 2 * shard), BF16)
    scratch = []
    if reads:
        operands += [gate_w, up_w]
        in_specs += [in_hbm()] * 2
        out_specs += [whole()]
        out_shape += [jax.ShapeDtypeStruct((tokens, depth), F32)]
        scratch += [held, pltpu.VMEM((2 * shard, tokens), BF16), pltpu.SemaphoreType.DMA((2, parts))]
    if writes:
        operands += [rows_t]
        in_specs += [whole()]
        out_specs += [in_hbm()] * 2
        out_shape += [jax.ShapeDtypeStruct((depth, units), BF16)] * 2
        scratch += [held, pltpu.SemaphoreType.DMA((2, parts))]
    if reads and not first:
        aliases[len(operands)] = 0
        operands += [total]
        in_specs += [whole()]
    if writes and not first:
        aliases.update({len(operands) + n: len(out_shape) - 2 + n for n in range(2)})
        operands += grads
        in_specs += [in_hbm()] * 2
    got = list(
        pl.pallas_call(
            functools.partial(both_body, parts, first, reads, writes),
            in_specs=in_specs,
            out_specs=out_specs,
            out_shape=out_shape,
            scratch_shapes=scratch,
            input_output_aliases=aliases,
            cost_estimate=cost(4 * (reads + writes) * tokens * depth * shard, 4 * (reads + writes) * depth * shard),
            compiler_params=params(),
            name="_".join(["input"] * reads + ["weights"] * writes),
        )(*operands)
    )
    return got.pop(0) if reads else total, got if writes else grads


def shards(loop, width, inputs, gate_weight, up_weight, down_weight, out_grad):
    hidden_dev = gate_weight.shape[1]
    shard = hidden_dev // width
    chips = loop // 2
    own_rows = inputs.shape[0]

    z_perm = ring_perm(width)
    y_perm = [(2 * a + core, 2 * b + core) for a, b in ring_perm(chips) for core in (0, 1)]
    core_perm = [(k, k ^ 1) for k in range(loop)]

    def gather_core(mine):
        return jnp.concatenate(mine + [lax.ppermute(m, "loop", core_perm) for m in mine], axis=0)

    def scatter_chips(mine):
        slots = [mine[k * own_rows : (k + 1) * own_rows] for k in range(chips)]
        return ring_scatter(slots, "loop", y_perm, chips).astype(BF16)

    def scatter_core(total):
        half = chips * own_rows
        return total[:half] + lax.ppermute(total[half:], "loop", core_perm)

    place = ring_place(lax.axis_index("width"), width)
    places = lax.rem(place + width - jnp.arange(width, dtype=jnp.int32), jnp.int32(width))

    def hop(sent):
        return lax.ppermute(sent, "width", z_perm)

    def add(got, term):
        return got.astype(F32) + term

    def slot_of(array, slot):
        return lax.dynamic_slice_in_dim(array, places[slot] * shard, shard, axis=1)

    def pre_of(slot, rows):
        return partial_pre(places[slot : slot + 1], rows, gate_weight, up_weight, shard, F32)

    gate_held, up_held = load(places[1:2], gate_weight, up_weight, shard)
    mine = ring_gather(inputs, "loop", y_perm, chips)
    out_grad, mine[-1] = together(out_grad, mine[-1])
    gathered = gather_core(mine)
    gate_first, up_first = matmul(gathered, gate_held).astype(BF16), matmul(gathered, up_held).astype(BF16)
    gate, up = hop(gate_first), hop(up_first)
    rows, gate_first, up_first = together(gathered, gate_first, up_first)
    slots = [(k + 1) % width for k in range(width)]
    terms = [None] * width
    terms[slots[1]] = pre_of(slots[1], rows)
    piece = gather_core(ring_gather(out_grad, "loop", y_perm, chips))
    piece, *terms[slots[1]] = together(piece, *terms[slots[1]])
    grad_n = {1: partial_hidden_grad(places[1:2], piece, down_weight, shard)[0]}
    gate, up = add(gate, terms[slots[1]][0]).astype(BF16), add(up, terms[slots[1]][1]).astype(BF16)
    if width > 2:
        rows, piece, gate, up = together(rows, piece, gate, up)
    for slot in slots[2:3]:
        terms[slot] = pre_of(slot, rows)
        piece, *terms[slot] = together(piece, *terms[slot])
    order = jnp.concatenate([places[2:], places[:1]])
    grad_n.update(zip(slots[1:], partial_hidden_grad(order, piece, down_weight, shard)))
    rows, grad_n[slots[1]] = together(rows, grad_n[slots[1]])
    for slot in slots[3:]:
        terms[slot] = pre_of(slot, rows)

    sent = grad_n[1].astype(BF16)
    for h in range(1, width - 1):
        got = hop(sent)
        gate, up = hop(gate), hop(up)
        if h < width - 2:
            gate, up = add(gate, terms[slots[h + 1]][0]).astype(BF16), add(up, terms[slots[h + 1]][1]).astype(BF16)
        sent = add(got, grad_n[h + 1]).astype(BF16)
    gate, up = add(gate, terms[0][0]), add(up, terms[0][1])
    sig = jax.nn.sigmoid(gate)
    sent, hidden_own = together(sent, (gate * sig * up).astype(BF16))
    hidden_grad = add(hop(sent), grad_n[0])
    hidden = [hidden_own, hop(hidden_own)]

    rows_t = turn(gathered)
    down = down_shard(places[:1], hidden[0], down_weight, piece, None)
    pre_gate = (hidden_grad * up * sig * (1.0 + gate * (1.0 - sig))).astype(BF16)
    pre_up = (hidden_grad * gate * sig).astype(BF16)
    pre = [jnp.concatenate([pre_gate, pre_up], axis=1)]
    pre[0], down[0], hidden[1] = together(pre[0], down[0], hidden[1])
    weights = gate_weight, up_weight, rows_t
    total, grads = None, None
    for k in range(width - 1):
        pre.append(hop(pre[k]))
        total, grads = input_and_weights(places[k : k + 1], pre[k], *weights, total, grads)
        if k < width - 2:
            hidden[k + 1], total = together(hidden[k + 1], total)
            hidden.append(hop(hidden[k + 1]))
        down = down_shard(places[k + 1 : k + 2], hidden[k + 1], down_weight, piece, down)
        if k < width - 2:
            pre[k + 1], total, down[0] = together(pre[k + 1], total, down[0])
            if k == width - 3:
                pre[k + 1], hidden[k + 2] = together(pre[k + 1], hidden[k + 2])
    here = places[width - 1 :]
    last, total, down[0] = together(pre[-1], total, down[0])
    output_mine = scatter_core(down[0])
    total, _ = input_and_weights(here, last, *weights, total, grads, writes=False)
    input_mine = scatter_core(total)
    last, total, output_mine = together(last, total, output_mine)
    output = scatter_chips(output_mine)
    _, (gate_grad, up_grad) = input_and_weights(here, last, *weights, total, grads, reads=False)
    input_grad = scatter_chips(input_mine)
    down_grad = down[1]
    return (output, input_grad, gate_grad, up_grad, down_grad)


def plain(inputs, gate_weight, up_weight, down_weight, out_grad):
    gathered = lax.all_gather(inputs, "loop", axis=0, tiled=True)
    gate = lax.psum(matmul(gathered, gate_weight), "width")
    up = lax.psum(matmul(gathered, up_weight), "width")
    sig = jax.nn.sigmoid(gate)
    hidden = (gate * sig * up).astype(BF16)
    output = lax.psum_scatter(matmul(hidden, down_weight), "loop", scatter_dimension=0, tiled=True).astype(BF16)
    piece = lax.all_gather(out_grad, "loop", axis=0, tiled=True)
    down_grad = contract_rows(hidden, piece).astype(BF16)
    hidden_grad = lax.psum(contract_cols(piece, down_weight), "width")
    pre_gate = (hidden_grad * up * sig * (1.0 + gate * (1.0 - sig))).astype(BF16)
    pre_up = (hidden_grad * gate * sig).astype(BF16)
    input_grad = lax.psum_scatter(
        contract_cols(pre_gate, gate_weight) + contract_cols(pre_up, up_weight),
        "loop",
        scatter_dimension=0,
        tiled=True,
    ).astype(BF16)
    gate_grad = contract_rows(gathered, pre_gate).astype(BF16)
    up_grad = contract_rows(gathered, pre_up).astype(BF16)
    return (output, input_grad, gate_grad, up_grad, down_grad)


def solution(mesh):
    loop, width = mesh.shape["loop"], mesh.shape["width"]

    def layer(*arrays):
        units = arrays[1].shape[1]
        if units % (width * LANES) or loop % 2 or width < 2:
            return plain(*arrays)
        return shards(loop, width, *arrays)

    in_specs = (
        P(("groups", "loop"), "width"),
        P("width", "loop"),
        P("width", "loop"),
        P("loop", "width"),
        P(("groups", "loop"), "width"),
    )
    out_specs = (
        P(("groups", "loop"), "width"),
        P(("groups", "loop"), "width"),
        P(("groups", "width"), "loop"),
        P(("groups", "width"), "loop"),
        P(("groups", "loop"), "width"),
    )
    return jax.shard_map(layer, mesh=mesh, in_specs=in_specs, out_specs=out_specs, check_vma=False)
```

```python
import functools

import jax
import jax.numpy as jnp
from jax import lax
from jax.experimental import pallas as pl
from jax.experimental.pallas import tpu as pltpu
from jax.sharding import PartitionSpec as P

BF16 = jnp.bfloat16
F32 = jnp.float32
LANES = 128
MIB = 1024 * 1024
KERNEL_VMEM = 46 * MIB


def contract_rows(left, right):
    return lax.dot_general(left, right, (((0,), (0,)), ((), ())), preferred_element_type=F32)


def contract_cols(left, right):
    return lax.dot_general(left, right, (((1,), (1,)), ((), ())), preferred_element_type=F32)


def matmul(left, right):
    return jnp.dot(left, right, preferred_element_type=F32)


def block_of(size, most):
    return max(b for b in range(LANES, most + 1, LANES) if size % b == 0)


def ring_order(n):
    return [0] + list(range(1, n, 2)) + [k for k in range(n - 1, 1, -1) if k % 2 == 0]


def ring_perm(n):
    order = ring_order(n)
    return [(order[k], order[(k + 1) % n]) for k in range(n)]


def ring_place(index, n):
    order = ring_order(n)
    place = jnp.int32(0)
    for k in range(n):
        place = jnp.where(index == order[k], k, place)
    return place.astype(jnp.int32)


def ring_gather(own, axis, perm, n):
    slots = [own]
    for _ in range(n - 1):
        slots.append(lax.ppermute(slots[-1], axis, perm))
    return slots


def ring_scatter(slots, axis, perm, n):
    total = slots[1 % n]
    for h in range(1, n):
        got = lax.ppermute(total.astype(BF16), axis, perm)
        total = got.astype(F32) + slots[(h + 1) % n]
    return total


def together(*arrays):
    return lax.optimization_barrier(list(arrays))


def params():
    return pltpu.CompilerParams(vmem_limit_bytes=KERNEL_VMEM)


def cost(flops, moved):
    return pl.CostEstimate(flops=flops // 64, bytes_accessed=moved // 64, transcendentals=0)


def whole():
    return pl.BlockSpec(memory_space=pltpu.VMEM)


def in_hbm():
    return pl.BlockSpec(memory_space=pltpu.HBM)


def number():
    return pl.BlockSpec(memory_space=pltpu.SMEM)


def copies(blocks, held, sems):
    return [pltpu.make_async_copy(block, held.at[k], sems.at[k]) for k, block in enumerate(blocks)]


def start(*lists):
    for group in zip(*lists):
        for copy in group:
            copy.start()


def columns_of(place, shard):
    return pl.ds(pl.multiple_of(place * shard, LANES), shard)


def load_body(parts, place, gate_w, up_w, gate_held, up_held, sems):
    depth, shard = gate_held.shape
    step, columns = depth // parts, columns_of(place[0], shard)
    loads = []
    for n, (source, held) in enumerate(((gate_w, gate_held), (up_w, up_held))):
        for k in range(parts):
            here = pl.ds(k * step, step)
            loads.append(pltpu.make_async_copy(source.at[here, columns], held.at[here], sems.at[n, k]))
            loads[-1].start()
    for copy in loads:
        copy.wait()


def load(place, gate_w, up_w, shard):
    parts, depth = 4, gate_w.shape[0]
    return pl.pallas_call(
        functools.partial(load_body, parts),
        in_specs=[number(), in_hbm(), in_hbm()],
        out_specs=[whole()] * 2,
        out_shape=[jax.ShapeDtypeStruct((depth, shard), gate_w.dtype)] * 2,
        scratch_shapes=[pltpu.SemaphoreType.DMA((2, parts))],
        cost_estimate=cost(0, 4 * depth * shard),
        compiler_params=params(),
        name="load",
    )(place, gate_w, up_w)


def pre_body(parts, place, rows, gate_w, up_w, gate, up, gate_held, up_held, gate_sum, up_sum, sems):
    depth, shard = gate_held.shape[1:]
    columns = columns_of(place[0], shard)
    here = [pl.ds(k * depth, depth) for k in range(parts)]
    gate_in = copies([gate_w.at[h, columns] for h in here], gate_held, sems.at[0])
    up_in = copies([up_w.at[h, columns] for h in here], up_held, sems.at[1])
    start(gate_in, up_in)
    for k in range(parts):
        part = rows[:, k * depth : (k + 1) * depth]
        gate_in[k].wait()
        up_in[k].wait()
        values = matmul(part, gate_held[k]), matmul(part, up_held[k])
        for value, total, out in zip(values, (gate_sum, up_sum), (gate, up)):
            if k:
                value += total[...]
            if k < parts - 1:
                total[...] = value
            else:
                out[...] = value.astype(out.dtype)


def partial_pre(place, rows, gate_w, up_w, shard, dtype):
    tokens, depth = rows.shape
    parts = depth // block_of(depth, 512)
    held = pltpu.VMEM((parts, depth // parts, shard), BF16)
    return pl.pallas_call(
        functools.partial(pre_body, parts),
        in_specs=[number(), whole(), in_hbm(), in_hbm()],
        out_specs=[whole()] * 2,
        out_shape=[jax.ShapeDtypeStruct((tokens, shard), dtype)] * 2,
        scratch_shapes=[held, held]
        + [pltpu.VMEM((tokens, shard), F32)] * 2
        + [pltpu.SemaphoreType.DMA((2, parts))],
        cost_estimate=cost(4 * tokens * depth * shard, 4 * depth * shard),
        compiler_params=params(),
        name="partial_pre",
    )(place, rows, gate_w, up_w)


def grad_body(count, places, rows, down_w, *rest):
    totals, (held, rows_t, sems) = rest[:count], rest[count:]
    shard = held.shape[1]
    loads = copies(
        [down_w.at[pl.ds(pl.multiple_of(places[j] * shard, LANES), shard)] for j in range(count)], held, sems
    )
    start(loads)
    rows_t[...] = rows[...].T
    half = shard // 2
    for j in range(count):
        loads[j].wait()
        low, high = matmul(held[j, :half], rows_t[...]), matmul(held[j, half:], rows_t[...])
        totals[j][...] = jnp.concatenate([low, high], axis=0).T


def partial_hidden_grad(places, rows, down_w, shard):
    count, (tokens, depth) = places.shape[0], rows.shape
    return list(
        pl.pallas_call(
            functools.partial(grad_body, count),
            in_specs=[number(), whole(), in_hbm()],
            out_specs=[whole()] * count,
            out_shape=[jax.ShapeDtypeStruct((tokens, shard), F32)] * count,
            scratch_shapes=[
                pltpu.VMEM((count, shard, depth), BF16),
                pltpu.VMEM((depth, tokens), BF16),
                pltpu.SemaphoreType.DMA((count,)),
            ],
            cost_estimate=cost(2 * count * tokens * depth * shard, 2 * count * depth * shard),
            compiler_params=params(),
            name="partial_hidden_grad",
        )(places, rows, down_w)
    )


def down_body(parts, first, place, hidden, down_w, rows, *rest):
    total, grad, held, made, hidden_t, in_sems, out_sems = rest[-7:]
    shard, step = held.shape[1:]
    units = columns_of(place[0], shard)
    here = [pl.ds(k * step, step) for k in range(parts)]
    loads = copies([down_w.at[units, h] for h in here], held, in_sems)
    start(loads)
    hidden_t[...] = hidden[...].T
    stores = []
    for k in range(parts):
        span = slice(k * step, (k + 1) * step)
        made[k] = matmul(hidden_t[...], rows[:, span]).astype(BF16)
        stores.append(pltpu.make_async_copy(made.at[k], grad.at[units, here[k]], out_sems.at[k]))
        stores[k].start()
        loads[k].wait()
        value = matmul(hidden[...], held[k])
        total[:, span] = value if first else rest[0][:, span] + value
    for store in stores:
        store.wait()


def down_shard(place, hidden, down_w, rows, before):
    tokens, shard = hidden.shape
    units, depth = down_w.shape
    step = block_of(depth, 512)
    parts = depth // step
    first = before is None
    held = pltpu.VMEM((parts, shard, step), BF16)
    return list(
        pl.pallas_call(
            functools.partial(down_body, parts, first),
            in_specs=[number(), whole(), in_hbm(), whole()] + ([] if first else [whole(), in_hbm()]),
            out_specs=[whole(), in_hbm()],
            out_shape=[
                jax.ShapeDtypeStruct((tokens, depth), F32),
                jax.ShapeDtypeStruct((units, depth), BF16),
            ],
            scratch_shapes=[held, held, pltpu.VMEM((shard, tokens), BF16)] + [pltpu.SemaphoreType.DMA((parts,))] * 2,
            input_output_aliases={} if first else {4: 0, 5: 1},
            cost_estimate=cost(4 * tokens * depth * shard, 4 * depth * shard),
            compiler_params=params(),
            name="down_shard",
        )(place, hidden, down_w, rows, *([] if first else before))
    )


def both_body(parts, first, writes, place, pre_gate, pre_up, gate_w, up_w, *rest):
    rest = list(rest)
    rows_t = rest.pop(0) if writes else None
    before = None if first else rest.pop(0)
    if writes and not first:
        del rest[:2]
    total = rest.pop(0)
    grads = [rest.pop(0) for _ in range(2)] if writes else []
    held, turned, in_sems = rest[:3]
    step, shard = held.shape[1], held.shape[2] // 2
    half, columns = step // 2, columns_of(place[0], shard)
    here = [pl.ds(k * step, step) for k in range(parts)]
    sides = pl.ds(0, shard), pl.ds(shard, shard)
    loads = [
        [
            pltpu.make_async_copy(source.at[h, columns], held.at[k, :, sides[n]], in_sems.at[n, k])
            for n, source in enumerate((gate_w, up_w))
        ]
        for k, h in enumerate(here)
    ]
    start(*zip(*loads))
    turned[:shard] = pre_gate[...].T
    turned[shard:] = pre_up[...].T
    if writes:
        made, flat, out_sems = rest[3:]
        flat[:, :shard] = pre_gate[...]
        flat[:, shard:] = pre_up[...]
    stores = []
    for k in range(parts):
        span = slice(k * step, (k + 1) * step)
        if writes:
            low, high = (matmul(rows_t[pl.ds(k * step + n * half, half)], flat[...]) for n in range(2))
            made[k, :half] = low.astype(BF16)
            made[k, half:] = high.astype(BF16)
            for n in range(2):
                stores.append(
                    pltpu.make_async_copy(made.at[k, :, sides[n]], grads[n].at[here[k], columns], out_sems.at[n, k])
                )
                stores[-1].start()
        for n in range(2):
            loads[k][n].wait()
        low, high = matmul(held[k, :half], turned[...]), matmul(held[k, half:], turned[...])
        value = jnp.concatenate([low, high], axis=0).T
        total[:, span] = value if first else before[:, span] + value
    for store in stores:
        store.wait()


def input_and_weights(place, pre_gate, pre_up, gate_w, up_w, rows_t, total, grads, writes=True):
    tokens, shard = pre_gate.shape
    depth, units = gate_w.shape
    step = block_of(depth, 512)
    parts = depth // step
    first = total is None
    operands, in_specs = [place, pre_gate, pre_up, gate_w, up_w], [number(), whole(), whole(), in_hbm(), in_hbm()]
    out_specs, out_shape, aliases = [whole()], [jax.ShapeDtypeStruct((tokens, depth), F32)], {}
    held = pltpu.VMEM((parts, step, 2 * shard), BF16)
    scratch = [held, pltpu.VMEM((2 * shard, tokens), BF16), pltpu.SemaphoreType.DMA((2, parts))]
    if writes:
        operands += [rows_t]
        in_specs += [whole()]
        out_specs += [in_hbm()] * 2
        out_shape += [jax.ShapeDtypeStruct((depth, units), BF16)] * 2
        scratch += [held, pltpu.VMEM((tokens, 2 * shard), BF16), pltpu.SemaphoreType.DMA((2, parts))]
    if not first:
        aliases[len(operands)] = 0
        operands += [total]
        in_specs += [whole()]
        if writes:
            aliases.update({len(operands): 1, len(operands) + 1: 2})
            operands += grads
            in_specs += [in_hbm()] * 2
    got = pl.pallas_call(
        functools.partial(both_body, parts, first, writes),
        in_specs=in_specs,
        out_specs=out_specs,
        out_shape=out_shape,
        scratch_shapes=scratch,
        input_output_aliases=aliases,
        cost_estimate=cost(8 * tokens * depth * shard, 8 * depth * shard),
        compiler_params=params(),
        name="input_and_weights" if writes else "input_shard",
    )(*operands)
    return got[0], list(got[1:]) if writes else grads


def turn_body(source, out):
    out[...] = source[...].T


def turn(source):
    rows, cols = source.shape
    return pl.pallas_call(
        turn_body,
        in_specs=[whole()],
        out_specs=whole(),
        out_shape=jax.ShapeDtypeStruct((cols, rows), source.dtype),
        cost_estimate=cost(0, 4 * source.size),
        compiler_params=params(),
        name="turn",
    )(source)


def weight_body(parts, place, pre, rows_t, *rest):
    grad, made, sems = rest[-3:]
    step, shard = made.shape[1:]
    half, columns = step // 2, columns_of(place[0], shard)
    stores = []
    for k in range(parts):
        low, high = (matmul(rows_t[pl.ds(k * step + n * half, half)], pre[...]) for n in range(2))
        made[k, :half] = low.astype(BF16)
        made[k, half:] = high.astype(BF16)
        stores.append(pltpu.make_async_copy(made.at[k], grad.at[pl.ds(k * step, step), columns], sems.at[k]))
        stores[k].start()
    for store in stores:
        store.wait()


def weight_shard(place, pre, rows_t, units, before):
    tokens, shard = pre.shape
    depth = rows_t.shape[0]
    step = block_of(depth, 512)
    parts = depth // step
    first = before is None
    return pl.pallas_call(
        functools.partial(weight_body, parts),
        in_specs=[number(), whole(), whole()] + ([] if first else [in_hbm()]),
        out_specs=in_hbm(),
        out_shape=jax.ShapeDtypeStruct((depth, units), BF16),
        scratch_shapes=[pltpu.VMEM((parts, step, shard), BF16), pltpu.SemaphoreType.DMA((parts,))],
        input_output_aliases={} if first else {3: 0},
        cost_estimate=cost(2 * tokens * depth * shard, 2 * depth * shard),
        compiler_params=params(),
        name="weight_shard",
    )(place, pre, rows_t, *([] if first else [before]))


def shards(loop, width, inputs, gate_weight, up_weight, down_weight, out_grad):
    hidden_dev = gate_weight.shape[1]
    shard = hidden_dev // width
    chips = loop // 2
    own_rows = inputs.shape[0]

    z_perm = ring_perm(width)
    y_perm = [(2 * a + core, 2 * b + core) for a, b in ring_perm(chips) for core in (0, 1)]
    core_perm = [(k, k ^ 1) for k in range(loop)]

    def gather_core(mine):
        return jnp.concatenate(mine + [lax.ppermute(m, "loop", core_perm) for m in mine], axis=0)

    def scatter_chips(mine):
        slots = [mine[k * own_rows : (k + 1) * own_rows] for k in range(chips)]
        return ring_scatter(slots, "loop", y_perm, chips).astype(BF16)

    def scatter_core(total):
        half = chips * own_rows
        return total[:half] + lax.ppermute(total[half:], "loop", core_perm)

    place = ring_place(lax.axis_index("width"), width)
    places = lax.rem(place + width - jnp.arange(width, dtype=jnp.int32), jnp.int32(width))

    def hop(sent):
        return lax.ppermute(sent, "width", z_perm)

    def add(got, term):
        return got.astype(F32) + term

    def slot_of(array, slot):
        return lax.dynamic_slice_in_dim(array, places[slot] * shard, shard, axis=1)

    def pre_of(slot, rows):
        return partial_pre(places[slot : slot + 1], rows, gate_weight, up_weight, shard, F32)

    gate_held, up_held = load(places[1:2], gate_weight, up_weight, shard)
    mine = ring_gather(inputs, "loop", y_perm, chips)
    out_grad, mine[-1] = together(out_grad, mine[-1])
    gathered = gather_core(mine)
    gate_first, up_first = matmul(gathered, gate_held).astype(BF16), matmul(gathered, up_held).astype(BF16)
    gate, up = hop(gate_first), hop(up_first)
    rows, gate_first, up_first = together(gathered, gate_first, up_first)
    slots = [(k + 1) % width for k in range(width)]
    terms = [None] * width
    terms[slots[1]] = pre_of(slots[1], rows)
    piece = gather_core(ring_gather(out_grad, "loop", y_perm, chips))
    piece, *terms[slots[1]] = together(piece, *terms[slots[1]])
    grad_n = {1: partial_hidden_grad(places[1:2], piece, down_weight, shard)[0]}
    gate, up = add(gate, terms[slots[1]][0]).astype(BF16), add(up, terms[slots[1]][1]).astype(BF16)
    if width > 2:
        rows, piece, gate, up = together(rows, piece, gate, up)
    for slot in slots[2:3]:
        terms[slot] = pre_of(slot, rows)
        piece, *terms[slot] = together(piece, *terms[slot])
    order = jnp.concatenate([places[2:], places[:1]])
    grad_n.update(zip(slots[1:], partial_hidden_grad(order, piece, down_weight, shard)))
    rows, grad_n[slots[1]] = together(rows, grad_n[slots[1]])
    for slot in slots[3:]:
        terms[slot] = pre_of(slot, rows)

    sent = grad_n[1].astype(BF16)
    for h in range(1, width - 1):
        got = hop(sent)
        gate, up = hop(gate), hop(up)
        if h < width - 2:
            gate, up = add(gate, terms[slots[h + 1]][0]).astype(BF16), add(up, terms[slots[h + 1]][1]).astype(BF16)
        sent = add(got, grad_n[h + 1]).astype(BF16)
    gate, up = add(gate, terms[0][0]), add(up, terms[0][1])
    sig = jax.nn.sigmoid(gate)
    sent, hidden_own = together(sent, (gate * sig * up).astype(BF16))
    hidden_grad = add(hop(sent), grad_n[0])
    hidden = [hidden_own, hop(hidden_own)]

    rows_t = turn(gathered)
    down = down_shard(places[:1], hidden[0], down_weight, piece, None)
    pre_gate = [(hidden_grad * up * sig * (1.0 + gate * (1.0 - sig))).astype(BF16)]
    pre_up = [(hidden_grad * gate * sig).astype(BF16)]
    pre_gate[0], down[0] = together(pre_gate[0], down[0])
    total, grads = None, None
    for k in range(width - 1):
        pre_gate.append(hop(pre_gate[k]))
        pre_up.append(hop(pre_up[k]))
        if k < width - 3:
            hidden.append(hop(hidden[k + 1]))
        args = places[k : k + 1], pre_gate[k], pre_up[k], gate_weight, up_weight, rows_t, total, grads
        total, grads = input_and_weights(*args)
        if k < width - 2:
            down = down_shard(places[k + 1 : k + 2], hidden[k + 1], down_weight, piece, down)
            pre_gate[k + 1], total = together(pre_gate[k + 1], total)
            pre_up[k + 1], down[0] = together(pre_up[k + 1], down[0])
    if width > 2:
        hidden[-1], total = together(hidden[-1], total)
        hidden.append(hop(hidden[-1]))
    here = places[width - 1 :]
    gate_grad = weight_shard(here, pre_gate[-1], rows_t, hidden_dev, grads[0])
    pre_up[-1], gate_grad = together(pre_up[-1], gate_grad)
    total, _ = input_and_weights(
        here, pre_gate[-1], pre_up[-1], gate_weight, up_weight, rows_t, total, grads, writes=False
    )
    hidden[-1], total = together(hidden[-1], total)
    input_mine = scatter_core(total)
    down = down_shard(here, hidden[-1], down_weight, piece, down)
    output_mine = scatter_core(down[0])
    pre_up[-1], output_mine = together(pre_up[-1], output_mine)
    input_grad, output = scatter_chips(input_mine), scatter_chips(output_mine)
    up_grad = weight_shard(here, pre_up[-1], rows_t, hidden_dev, grads[1])
    down_grad = down[1]
    return (output, input_grad, gate_grad, up_grad, down_grad)


def plain(inputs, gate_weight, up_weight, down_weight, out_grad):
    gathered = lax.all_gather(inputs, "loop", axis=0, tiled=True)
    gate = lax.psum(matmul(gathered, gate_weight), "width")
    up = lax.psum(matmul(gathered, up_weight), "width")
    sig = jax.nn.sigmoid(gate)
    hidden = (gate * sig * up).astype(BF16)
    output = lax.psum_scatter(matmul(hidden, down_weight), "loop", scatter_dimension=0, tiled=True).astype(BF16)
    piece = lax.all_gather(out_grad, "loop", axis=0, tiled=True)
    down_grad = contract_rows(hidden, piece).astype(BF16)
    hidden_grad = lax.psum(contract_cols(piece, down_weight), "width")
    pre_gate = (hidden_grad * up * sig * (1.0 + gate * (1.0 - sig))).astype(BF16)
    pre_up = (hidden_grad * gate * sig).astype(BF16)
    input_grad = lax.psum_scatter(
        contract_cols(pre_gate, gate_weight) + contract_cols(pre_up, up_weight),
        "loop",
        scatter_dimension=0,
        tiled=True,
    ).astype(BF16)
    gate_grad = contract_rows(gathered, pre_gate).astype(BF16)
    up_grad = contract_rows(gathered, pre_up).astype(BF16)
    return (output, input_grad, gate_grad, up_grad, down_grad)


def solution(mesh):
    loop, width = mesh.shape["loop"], mesh.shape["width"]

    def layer(*arrays):
        units = arrays[1].shape[1]
        if units % (width * LANES) or loop % 2 or width < 2:
            return plain(*arrays)
        return shards(loop, width, *arrays)

    in_specs = (
        P(("groups", "loop"), "width"),
        P("width", "loop"),
        P("width", "loop"),
        P("loop", "width"),
        P(("groups", "loop"), "width"),
    )
    out_specs = (
        P(("groups", "loop"), "width"),
        P(("groups", "loop"), "width"),
        P(("groups", "width"), "loop"),
        P(("groups", "width"), "loop"),
        P(("groups", "loop"), "width"),
    )
    return jax.shard_map(layer, mesh=mesh, in_specs=in_specs, out_specs=out_specs, check_vma=False)
```
